512 devices in a mesh: ia: 8 (over y, core), ao: 8 (over x, z_hi), ta: 8 (over z_lo).
Axes of the slice: x: 4, y: 4, z: 16 (z_hi: 2, z_lo: 8; z = z_hi * 8 + z_lo), core: 2. Of those that a mesh axis runs over, the one named last changes fastest.
Arguments:
- inputs: bfloat16 [768, 8192], P(('ao', 'ta'), 'ia'), may hold values from -6 to 6
- out_grad: bfloat16 [768, 8192], P(('ao', 'ta'), 'ia'), may hold values from -6 to 6
- preact: bfloat16 [768, 16384], P('ia', ('ao', 'ta')), may hold values from -6 to 6
- up_weight: bfloat16 [8192, 16384], P('ia', ('ao', 'ta')), may hold values from -0.0625 to 0.0625
- down_weight: bfloat16 [16384, 8192], P(('ao', 'ta'), 'ia'), may hold values from -0.046875 to 0.046875
Outputs:
- input_grad: bfloat16 [768, 8192], P(('ao', 'ta'), 'ia')
- up_grad: float32 [8192, 16384], P('ia', ('ao', 'ta'))
- down_grad: float32 [16384, 8192], P(('ao', 'ta'), 'ia')
The draws below stay inside these ranges and needn't reach their ends.
All inputs are finite; a program needn't handle non-finite values.
Results may differ from the reference program's by a relative error of at most 0.0049.
Values may be sent and summed in bfloat16 or wider, within the bound.
No kernel may reach another device: no remote copies, remote signals or barrier semaphores. Data moves between devices by JAX's collectives and lax.ppermute only.
A program may use at most 64 MiB of HBM per device.

```python
import math
import jax
import jax.numpy as jnp

D = 8192
FF = 16384
TOKENS = 768


def block_scale(stream_key, extent, pieces, smallest, top_value):
    loudness, own = 1.0, jax.random.fold_in(stream_key, 6)
    for position, shards_of in pieces:
        draws = jnp.exp(jax.random.uniform(jax.random.fold_in(own, position), (shards_of,), jnp.float32, smallest / len(pieces), top_value / len(pieces)))
        loudness = loudness * jnp.repeat(draws, extent[position] // shards_of).reshape([-1 if axis == position else 1 for axis in range(len(extent))])
    return loudness


def centred(stream_key, dims, spread, most, pieces=(), held_as=jnp.bfloat16):
    loudness = block_scale(stream_key, dims, pieces, -0.22, 0.18) if pieces else 1.0
    entries = jax.random.normal(stream_key, dims, jnp.float32) * spread * loudness
    return jnp.minimum(jnp.maximum(entries, -most), most).astype(held_as)


def setup_inputs(seed: int = 0) -> dict:
    seeds = jax.random.split(jax.random.key(seed), 6)
    return {
        "inputs": centred(seeds[0], (TOKENS, D), 1.0, 6.0, ((0, 64), (1, 8))),
        "out_grad": centred(seeds[1], (TOKENS, D), 0.5, 6.0, ((0, 64), (1, 8))),
        "preact": centred(seeds[2], (TOKENS, FF), 1.0, 6.0, ((0, 8), (1, 64))),
        "up_weight": centred(seeds[3], (D, FF), D ** -0.5, 0.0625, ((0, 8), (1, 64))),
        "down_weight": centred(seeds[4], (FF, D), FF ** -0.5, 0.046875, ((0, 64), (1, 8))),
    }


def gelu_parts(preact):
    value = preact.astype(jnp.float32)
    normal_cdf = 0.5 * (1.0 + jax.scipy.special.erf(value / math.sqrt(2.0)))
    density = jnp.exp(-0.5 * value * value) / math.sqrt(2.0 * math.pi)
    return (value * normal_cdf, normal_cdf + value * density)

def reference(inputs, out_grad, preact, up_weight, down_weight):
    hidden_grad = jnp.dot(out_grad, down_weight.T, preferred_element_type=jnp.float32)
    activ, slope = gelu_parts(preact)
    activ = activ.astype(jnp.bfloat16)
    pre_grad = (hidden_grad * slope).astype(jnp.bfloat16)
    up_grad = jnp.dot(inputs.T, pre_grad, preferred_element_type=jnp.float32)
    down_grad = jnp.dot(activ.T, out_grad, preferred_element_type=jnp.float32)
    input_grad = jnp.dot(pre_grad, up_weight.T, preferred_element_type=jnp.float32).astype(jnp.bfloat16)
    return (input_grad, up_grad, down_grad)
```

```python
import math

import jax
import jax.numpy as jnp
from jax import lax
from jax.sharding import Mesh, PartitionSpec as P

BF = jnp.bfloat16
F32 = jnp.float32


def gelu_parts(preact):
    value = preact.astype(F32)
    normal_cdf = 0.5 * (1.0 + jax.scipy.special.erf(value / math.sqrt(2.0)))
    density = jnp.exp(-0.5 * value * value) / math.sqrt(2.0 * math.pi)
    return (value * normal_cdf, normal_cdf + value * density)


def exchange(blocks, axis):
    return lax.all_to_all(blocks, axis, split_axis=0, concat_axis=0, tiled=False)


def spread(block, axis, n):
    return exchange(jnp.broadcast_to(block[None], (n,) + block.shape), axis)


def halves_down(block):
    lead, (rows, cols) = block.shape[:-2], block.shape[-2:]
    split = block.reshape(*lead, rows, 2, cols // 2)
    return jnp.swapaxes(split, -3, -2).reshape(*lead, rows * 2, cols // 2)


def halves_across(block):
    lead, (rows, cols) = block.shape[:-2], block.shape[-2:]
    split = block.reshape(*lead, 2, rows // 2, cols)
    return jnp.swapaxes(split, -3, -2).reshape(*lead, rows // 2, cols * 2)


def local(inputs, out_grad, preact, up_weight, down_weight):
    core = lax.axis_index("c")
    both = jnp.concatenate([halves_down(out_grad), halves_down(inputs)], axis=0)
    both = spread(both, "za", 4)
    rows = 24
    grads = halves_across(both[:, :rows]).reshape(48, 1024)
    ins = halves_across(both[:, rows:]).reshape(48, 1024)
    all_inputs = lax.all_gather(ins, ("x", "zb"), axis=0, tiled=True)
    grads = spread(grads, "zb", 4).reshape(192, 1024)
    all_grads = spread(grads, "x", 4).reshape(768, 1024)

    partial = jnp.einsum("td,fd->tf", all_grads, down_weight, preferred_element_type=F32)
    partial = partial.reshape(4, 4, 2, 24, 256)
    mine = lax.dynamic_index_in_dim(partial, core, axis=2, keepdims=False)
    theirs = lax.dynamic_index_in_dim(partial, 1 - core, axis=2, keepdims=False)
    pair = mine + lax.ppermute(theirs, "c", [(0, 1), (1, 0)])
    pair = exchange(pair.reshape(4, 96, 256), "y")
    hidden_grad = pair.sum(0)

    rows_first = preact.reshape(2, 4, 12, 256).transpose(1, 0, 2, 3).reshape(96, 256)
    activ, slope = gelu_parts(rows_first)
    own = jnp.stack([(hidden_grad * slope).astype(BF), activ.astype(BF)])
    own = spread(own, "y", 4)
    own = lax.all_gather(own, "c", axis=0, tiled=False)
    own = own.reshape(2, 4, 2, 4, 24, 256).transpose(2, 1, 3, 0, 4, 5).reshape(2, 768, 256)
    all_pregrad, all_activ = own[0], own[1]

    part = jnp.einsum("tf,df->td", all_pregrad, up_weight, preferred_element_type=F32)
    part = exchange(part.astype(BF).reshape(4, 192, 1024), "x")
    part = part.astype(F32).sum(0)
    part = exchange(part.astype(BF).reshape(4, 48, 1024), "zb")
    part = part.astype(F32).sum(0)
    part = exchange(halves_down(part.astype(BF).reshape(4, 12, 1024)), "za")
    input_grad = halves_across(part.astype(F32).sum(0)).astype(BF)

    down_grad = jnp.einsum("tf,td->fd", all_activ, all_grads, preferred_element_type=F32)
    up_grad = jnp.einsum("td,tf->df", all_inputs, all_pregrad, preferred_element_type=F32)
    return (input_grad, up_grad, down_grad)


def solution(mesh):
    fine = Mesh(mesh.devices.reshape(4, 2, 4, 4, 4), ("y", "c", "x", "za", "zb"))
    tokens, width = ("x", "za", "zb"), ("y", "c")
    return jax.shard_map(
        local,
        mesh=fine,
        in_specs=(
            P(tokens, width),
            P(tokens, width),
            P(width, tokens),
            P(width, tokens),
            P(tokens, width),
        ),
        out_specs=(P(tokens, width), P(width, tokens), P(tokens, width)),
        check_vma=False,
    )
```

```python
import math

import jax
import jax.numpy as jnp
from jax import lax
from jax.sharding import Mesh, PartitionSpec as P

BF = jnp.bfloat16
F32 = jnp.float32


def gelu_parts(preact):
    value = preact.astype(F32)
    normal_cdf = 0.5 * (1.0 + jax.scipy.special.erf(value / math.sqrt(2.0)))
    density = jnp.exp(-0.5 * value * value) / math.sqrt(2.0 * math.pi)
    return (value * normal_cdf, normal_cdf + value * density)


def exchange(blocks, axis):
    return lax.all_to_all(blocks, axis, split_axis=0, concat_axis=0, tiled=False)


def spread(block, axis, n=4):
    return exchange(jnp.broadcast_to(block[None], (n,) + block.shape), axis)


def halves_down(block):
    lead, (rows, cols) = block.shape[:-2], block.shape[-2:]
    split = block.reshape(*lead, rows, 2, cols // 2)
    return jnp.swapaxes(split, -3, -2).reshape(*lead, rows * 2, cols // 2)


def halves_across(block):
    lead, (rows, cols) = block.shape[:-2], block.shape[-2:]
    split = block.reshape(*lead, 2, rows // 2, cols)
    return jnp.swapaxes(split, -3, -2).reshape(*lead, rows // 2, cols * 2)


def gather_x(block):
    half = block.shape[0] // 2
    before = lax.ppermute(block, "x", shift(1))
    after = lax.ppermute(block, "x", shift(-1))
    far = jnp.concatenate(
        [lax.ppermute(before[:half], "x", shift(1)), lax.ppermute(after[half:], "x", shift(-1))]
    )
    return jnp.stack([block, after, far, before])


def shift(k):
    return [(i, (i + k) % 4) for i in range(4)]


def turn_by(blocks, start):
    twice = jnp.concatenate([blocks, blocks[:3]])
    return lax.dynamic_slice_in_dim(twice, start, 4, axis=0)


def local(inputs, out_grad, preact, up_weight, down_weight):
    core, at_x = lax.axis_index("c"), lax.axis_index("x")
    wide_down = lax.all_gather(down_weight, "x", axis=0, tiled=True).reshape(4, 256, 1024)
    both = jnp.concatenate([halves_down(out_grad), halves_down(inputs)], axis=0)
    both = spread(both, "za")
    both = halves_across(both.reshape(4, 2, 24, 512)).swapaxes(0, 1).reshape(96, 1024)
    both = spread(both, "zb").reshape(4, 2, 48, 1024).swapaxes(0, 1).reshape(2, 192, 1024)
    grads = both[0]

    rows_first = preact.reshape(2, 4, 12, 256).transpose(1, 0, 2, 3).reshape(96, 256)
    swap = [(4 * a + b, 4 * b + a) for a in range(4) for b in range(4)]
    turned = lax.ppermute(rows_first, ("y", "x"), swap)

    partial = jnp.einsum("td,xfd->xtf", grads, wide_down, preferred_element_type=F32)
    partial = partial.reshape(4, 4, 2, 24, 256)
    mine = lax.dynamic_index_in_dim(partial, core, axis=2, keepdims=False)
    theirs = lax.dynamic_index_in_dim(partial, 1 - core, axis=2, keepdims=False)
    pair = mine + lax.ppermute(theirs, "c", [(0, 1), (1, 0)])
    hidden_grad = exchange(pair.reshape(4, 96, 256), "y").sum(0)

    _, slope = gelu_parts(turned)
    activ, _ = gelu_parts(rows_first)
    own = spread(jnp.stack([(hidden_grad * slope).astype(BF), activ.astype(BF)]), "y")
    own = lax.all_gather(own, "c", axis=0, tiled=False).reshape(2, 4, 2, 4, 24, 256)
    own = own.transpose(2, 1, 3, 0, 4, 5).reshape(2, 4, 192, 256)
    pregrad, all_activ = turn_by(own[0], at_x), own[1]

    wide_up = gather_x(up_weight)
    part = jnp.einsum("xtf,xdf->td", pregrad, wide_up, preferred_element_type=F32)
    part = exchange(part.astype(BF).reshape(4, 48, 1024), "zb")
    part = part.astype(F32).sum(0)
    part = exchange(halves_down(part.astype(BF).reshape(4, 12, 1024)), "za")
    input_grad = halves_across(part.astype(F32).sum(0)).astype(BF)

    sent = [pregrad[0]] + [lax.ppermute(pregrad[k], "x", shift(k)) for k in (3, 2, 1)]
    all_pregrad = turn_by(jnp.stack(sent), (4 - at_x) % 4).reshape(768, 256)
    all_both = lax.all_gather(both.reshape(384, 1024), "x", axis=0, tiled=False)
    all_both = all_both.reshape(4, 2, 192, 1024)
    down_grad = jnp.einsum("xtf,xtd->fd", all_activ, all_both[:, 0], preferred_element_type=F32)
    up_grad = jnp.einsum(
        "xtd,xtf->df", all_both[:, 1], all_pregrad.reshape(4, 192, 256), preferred_element_type=F32
    )
    return (input_grad, up_grad, down_grad)


def solution(mesh):
    fine = Mesh(mesh.devices.reshape(4, 2, 4, 4, 4), ("y", "c", "x", "za", "zb"))
    tokens, width = ("x", "za", "zb"), ("y", "c")
    return jax.shard_map(
        local,
        mesh=fine,
        in_specs=(
            P(tokens, width),
            P(tokens, width),
            P(width, tokens),
            P(width, tokens),
            P(tokens, width),
        ),
        out_specs=(P(tokens, width), P(width, tokens), P(tokens, width)),
        check_vma=False,
    )
```

```python
import math

import jax
import jax.numpy as jnp
from jax import lax
from jax.sharding import Mesh, PartitionSpec as P

BF = jnp.bfloat16
F32 = jnp.float32


def gelu_parts(preact):
    value = preact.astype(F32)
    normal_cdf = 0.5 * (1.0 + jax.scipy.special.erf(value / math.sqrt(2.0)))
    density = jnp.exp(-0.5 * value * value) / math.sqrt(2.0 * math.pi)
    return (value * normal_cdf, normal_cdf + value * density)


def exchange(blocks, axis):
    return lax.all_to_all(blocks, axis, split_axis=0, concat_axis=0, tiled=False)


def spread(block, axis, n=4):
    return exchange(jnp.broadcast_to(block[None], (n,) + block.shape), axis)


def halves_down(block):
    lead, (rows, cols) = block.shape[:-2], block.shape[-2:]
    split = block.reshape(*lead, rows, 2, cols // 2)
    return jnp.swapaxes(split, -3, -2).reshape(*lead, rows * 2, cols // 2)


def halves_across(block):
    lead, (rows, cols) = block.shape[:-2], block.shape[-2:]
    split = block.reshape(*lead, 2, rows // 2, cols)
    return jnp.swapaxes(split, -3, -2).reshape(*lead, rows // 2, cols * 2)


def near_x(block):
    return lax.ppermute(block, "x", shift(1)), lax.ppermute(block, "x", shift(-1))


def far_x(before, after):
    half = before.shape[0] // 2
    return jnp.concatenate(
        [lax.ppermute(before[:half], "x", shift(1)), lax.ppermute(after[half:], "x", shift(-1))]
    )


def shift(k):
    return [(i, (i + k) % 4) for i in range(4)]


def turn_by(blocks, start):
    twice = jnp.concatenate([blocks, blocks[:3]])
    return lax.dynamic_slice_in_dim(twice, start, 4, axis=0)


def local(inputs, out_grad, preact, up_weight, down_weight):
    core, at_x = lax.axis_index("c"), lax.axis_index("x")
    wide_down = lax.all_gather(down_weight, "x", axis=0, tiled=True).reshape(4, 256, 1024)
    both = jnp.concatenate([halves_down(out_grad), halves_down(inputs)], axis=0)
    both = spread(both, "za")
    rows_first = preact.reshape(2, 4, 12, 256).transpose(1, 0, 2, 3).reshape(96, 256)
    swap = [(4 * a + b, 4 * b + a) for a in range(4) for b in range(4)]
    turned = lax.ppermute(rows_first, ("y", "x"), swap)
    before, after = near_x(up_weight)
    both, turned, before, after = lax.optimization_barrier((both, turned, before, after))
    both = halves_across(both.reshape(4, 2, 24, 512)).swapaxes(0, 1).reshape(2, 48, 1024)
    grads = spread(both[0], "zb").reshape(192, 1024)
    ins = spread(both[1], "zb").reshape(192, 1024)
    wide_up = jnp.stack([up_weight, after, far_x(before, after), before])
    grads, wide_up = lax.optimization_barrier((grads, wide_up))

    partial = jnp.einsum("td,xfd->xtf", grads, wide_down, preferred_element_type=F32)
    partial = partial.reshape(4, 4, 2, 24, 256)
    mine = lax.dynamic_index_in_dim(partial, core, axis=2, keepdims=False)
    theirs = lax.dynamic_index_in_dim(partial, 1 - core, axis=2, keepdims=False)
    pair = mine + lax.ppermute(theirs, "c", [(0, 1), (1, 0)])
    hidden_grad = exchange(pair.reshape(4, 96, 256), "y").sum(0)

    _, slope = gelu_parts(turned)
    activ, _ = gelu_parts(rows_first)
    own = spread(jnp.stack([(hidden_grad * slope).astype(BF), activ.astype(BF)]), "y")
    own = lax.all_gather(own, "c", axis=0, tiled=False).reshape(2, 4, 2, 4, 24, 256)
    own = own.transpose(2, 1, 3, 0, 4, 5).reshape(2, 4, 192, 256)
    pregrad, all_activ = turn_by(own[0], at_x), own[1]

    part = jnp.einsum("xtf,xdf->td", pregrad, wide_up, preferred_element_type=F32)
    part = exchange(part.astype(BF).reshape(4, 48, 1024), "zb")
    part = part.astype(F32).sum(0)
    part, pregrad = lax.optimization_barrier((part, pregrad))
    part = exchange(halves_down(part.astype(BF).reshape(4, 12, 1024)), "za")
    input_grad = halves_across(part.astype(F32).sum(0)).astype(BF)

    sent = [pregrad[0]] + [lax.ppermute(pregrad[k], "x", shift(k)) for k in (3, 2, 1)]
    all_pregrad = turn_by(jnp.stack(sent), (4 - at_x) % 4).reshape(768, 256)
    all_both = lax.all_gather(jnp.concatenate([grads, ins]), "x", axis=0, tiled=False)
    all_both = all_both.reshape(4, 2, 192, 1024)
    down_grad = jnp.einsum("xtf,xtd->fd", all_activ, all_both[:, 0], preferred_element_type=F32)
    up_grad = jnp.einsum(
        "xtd,xtf->df", all_both[:, 1], all_pregrad.reshape(4, 192, 256), preferred_element_type=F32
    )
    return (input_grad, up_grad, down_grad)


def solution(mesh):
    fine = Mesh(mesh.devices.reshape(4, 2, 4, 4, 4), ("y", "c", "x", "za", "zb"))
    tokens, width = ("x", "za", "zb"), ("y", "c")
    return jax.shard_map(
        local,
        mesh=fine,
        in_specs=(
            P(tokens, width),
            P(tokens, width),
            P(width, tokens),
            P(width, tokens),
            P(tokens, width),
        ),
        out_specs=(P(tokens, width), P(width, tokens), P(tokens, width)),
        check_vma=False,
    )
```

```python
import math

import jax
import jax.numpy as jnp
from jax import lax
from jax.sharding import Mesh, PartitionSpec as P

BF = jnp.bfloat16
F32 = jnp.float32


def gelu_parts(preact):
    value = preact.astype(F32)
    normal_cdf = 0.5 * (1.0 + jax.scipy.special.erf(value / math.sqrt(2.0)))
    density = jnp.exp(-0.5 * value * value) / math.sqrt(2.0 * math.pi)
    return (value * normal_cdf, normal_cdf + value * density)


def exchange(blocks, axis):
    return lax.all_to_all(blocks, axis, split_axis=0, concat_axis=0, tiled=False)


def spread(block, axis, n=4):
    return exchange(jnp.broadcast_to(block[None], (n,) + block.shape), axis)


def halves_down(block):
    lead, (rows, cols) = block.shape[:-2], block.shape[-2:]
    split = block.reshape(*lead, rows, 2, cols // 2)
    return jnp.swapaxes(split, -3, -2).reshape(*lead, rows * 2, cols // 2)


def halves_across(block):
    lead, (rows, cols) = block.shape[:-2], block.shape[-2:]
    split = block.reshape(*lead, 2, rows // 2, cols)
    return jnp.swapaxes(split, -3, -2).reshape(*lead, rows // 2, cols * 2)


def shift(k):
    return [(i, (i + k) % 4) for i in range(4)]


def turn_by(blocks, start):
    twice = jnp.concatenate([blocks, blocks[:3]])
    return lax.dynamic_slice_in_dim(twice, start, 4, axis=0)


def local(inputs, out_grad, preact, up_weight, down_weight):
    core, at_x = lax.axis_index("c"), lax.axis_index("x")
    up_rows = up_weight.reshape(4, 256, 256).swapaxes(0, 1).reshape(256, 1024)
    wide = lax.all_gather(jnp.concatenate([down_weight, up_rows]), "x", axis=0, tiled=False)
    wide_down, wide_up = wide[:, :256], wide[:, 256:].reshape(4, 256, 4, 256)

    both = jnp.concatenate([halves_down(out_grad), halves_down(inputs)], axis=0)
    both = spread(both, "za")
    rows_first = preact.reshape(2, 4, 12, 256).transpose(1, 0, 2, 3).reshape(96, 256)
    swap = [(4 * a + b, 4 * b + a) for a in range(4) for b in range(4)]
    turned = lax.ppermute(rows_first, ("y", "x"), swap)
    both, turned = lax.optimization_barrier((both, turned))
    both = halves_across(both.reshape(4, 2, 24, 512)).swapaxes(0, 1).reshape(96, 1024)
    both = spread(both, "zb").reshape(4, 2, 48, 1024).swapaxes(0, 1).reshape(2, 192, 1024)
    grads, ins = both[0], both[1]

    partial = jnp.einsum("td,xfd->xtf", grads, wide_down, preferred_element_type=F32)
    partial = partial.reshape(4, 4, 2, 24, 256)
    mine = lax.dynamic_index_in_dim(partial, core, axis=2, keepdims=False)
    theirs = lax.dynamic_index_in_dim(partial, 1 - core, axis=2, keepdims=False)
    pair = mine + lax.ppermute(theirs, "c", [(0, 1), (1, 0)])
    hidden_grad = exchange(pair.reshape(4, 96, 256), "y").sum(0)

    _, slope = gelu_parts(turned)
    activ, _ = gelu_parts(rows_first)
    own = spread(jnp.stack([(hidden_grad * slope).astype(BF), activ.astype(BF)]), "y")
    own = lax.all_gather(own, "c", axis=0, tiled=False).reshape(2, 4, 2, 4, 24, 256)
    own = own.transpose(2, 1, 3, 0, 4, 5).reshape(2, 4, 192, 256)
    pregrad, all_activ = own[0], own[1]

    part = jnp.einsum("xtf,xrkf->tkr", pregrad, wide_up, preferred_element_type=F32)
    part = exchange(part.astype(BF).reshape(4, 48, 1024), "zb")
    part = part.astype(F32).sum(0)
    part, pregrad = lax.optimization_barrier((part, pregrad))
    part = exchange(halves_down(part.astype(BF).reshape(4, 12, 1024)), "za")
    input_grad = halves_across(part.astype(F32).sum(0)).astype(BF)

    pregrad = turn_by(pregrad, at_x)
    sent = [pregrad[0]] + [lax.ppermute(pregrad[k], "x", shift(k)) for k in (3, 2, 1)]
    all_pregrad = turn_by(jnp.stack(sent), (4 - at_x) % 4)
    all_pregrad, all_activ = lax.optimization_barrier((all_pregrad, all_activ))
    all_both = lax.all_gather(both.reshape(384, 1024), "x", axis=0, tiled=False)
    all_both = all_both.reshape(4, 2, 192, 1024)
    down_grad = jnp.einsum("xtf,xtd->fd", all_activ, all_both[:, 0], preferred_element_type=F32)
    up_grad = jnp.einsum(
        "xtd,xtf->df", all_both[:, 1], all_pregrad, preferred_element_type=F32
    )
    return (input_grad, up_grad, down_grad)


def solution(mesh):
    fine = Mesh(mesh.devices.reshape(4, 2, 4, 4, 4), ("y", "c", "x", "za", "zb"))
    tokens, width = ("x", "za", "zb"), ("y", "c")
    return jax.shard_map(
        local,
        mesh=fine,
        in_specs=(
            P(tokens, width),
            P(tokens, width),
            P(width, tokens),
            P(width, tokens),
            P(tokens, width),
        ),
        out_specs=(P(tokens, width), P(width, tokens), P(tokens, width)),
        check_vma=False,
    )
```

```python
import math

import jax
import jax.numpy as jnp
from jax import lax
from jax.sharding import Mesh, PartitionSpec as P

BF = jnp.bfloat16
F32 = jnp.float32


def gelu_parts(preact):
    value = preact.astype(F32)
    normal_cdf = 0.5 * (1.0 + jax.scipy.special.erf(value / math.sqrt(2.0)))
    density = jnp.exp(-0.5 * value * value) / math.sqrt(2.0 * math.pi)
    return (value * normal_cdf, normal_cdf + value * density)


def exchange(blocks, axis):
    return lax.all_to_all(blocks, axis, split_axis=0, concat_axis=0, tiled=False)


def spread(block, axis, n=4):
    return exchange(jnp.broadcast_to(block[None], (n,) + block.shape), axis)


def halves_down(block):
    lead, (rows, cols) = block.shape[:-2], block.shape[-2:]
    split = block.reshape(*lead, rows, 2, cols // 2)
    return jnp.swapaxes(split, -3, -2).reshape(*lead, rows * 2, cols // 2)


def halves_across(block):
    lead, (rows, cols) = block.shape[:-2], block.shape[-2:]
    split = block.reshape(*lead, 2, rows // 2, cols)
    return jnp.swapaxes(split, -3, -2).reshape(*lead, rows // 2, cols * 2)


def shift(k):
    return [(i, (i + k) % 4) for i in range(4)]


def turn_by(blocks, start):
    twice = jnp.concatenate([blocks, blocks[:3]])
    return lax.dynamic_slice_in_dim(twice, start, 4, axis=0)


def local(inputs, out_grad, preact, up_weight, down_weight):
    core, at_x, at_y = lax.axis_index("c"), lax.axis_index("x"), lax.axis_index("y")
    up_rows = jnp.concatenate([up_weight[256 * k : 256 * (k + 1)] for k in range(4)], axis=1)
    wide = lax.all_gather(jnp.concatenate([down_weight, up_rows]), "x", axis=0, tiled=False)
    wide_down, wide_up = wide[:, :256], wide[:, 256:].reshape(4, 256, 4, 256)

    both = jnp.concatenate([halves_down(out_grad), halves_down(inputs)], axis=0)
    both = spread(both, "za")
    rows_first = preact.reshape(2, 4, 12, 256).transpose(1, 0, 2, 3).reshape(96, 256)
    turned = [
        lax.ppermute(
            rows_first,
            ("y", "x"),
            [(4 * a + b, 4 * ((b - k) % 4) + a) for a in range(4) for b in range(4)],
        )
        for k in range(4)
    ]
    both, turned = lax.optimization_barrier((both, turned))
    turned = turn_by(jnp.stack(turned), (4 - at_y) % 4)
    both = halves_across(both.reshape(4, 2, 24, 512)).swapaxes(0, 1).reshape(96, 1024)
    both = spread(both, "zb").reshape(4, 2, 48, 1024).swapaxes(0, 1).reshape(2, 192, 1024)
    grads = both[0]

    partial = jnp.einsum("td,xfd->xtf", grads, wide_down, preferred_element_type=F32)
    partial = partial.reshape(4, 4, 2, 24, 256)
    mine = lax.dynamic_index_in_dim(partial, core, axis=2, keepdims=False)
    theirs = lax.dynamic_index_in_dim(partial, 1 - core, axis=2, keepdims=False)
    pair = (mine + lax.ppermute(theirs, "c", [(0, 1), (1, 0)])).astype(BF).reshape(4, 96, 256)
    activ, _ = gelu_parts(rows_first)
    own = spread(jnp.concatenate([pair, activ.astype(BF)[None]]), "y")
    hidden_grad = own[:, :4].astype(F32).sum(0)
    _, slope = gelu_parts(turned)
    own = jnp.concatenate([(hidden_grad * slope).astype(BF), own[:, 4]])
    own = lax.all_gather(own, "c", axis=0, tiled=False).reshape(2, 2, 4, 4, 24, 256)
    own = own.transpose(1, 2, 3, 0, 4, 5).reshape(2, 4, 192, 256)
    pregrad, all_activ = own[0], own[1]

    part = jnp.einsum("xtf,xrkf->tkr", pregrad, wide_up, preferred_element_type=F32)
    part = part.astype(BF).reshape(4, 4, 12, 1024).swapaxes(0, 1)
    part = exchange(halves_down(part.reshape(16, 12, 1024)), ("za", "zb"))
    input_grad = halves_across(part.astype(F32).sum(0)).astype(BF)

    pregrad = turn_by(pregrad, at_x)
    sent = [pregrad[0]] + [lax.ppermute(pregrad[k], "x", shift(k)) for k in (3, 2, 1)]
    all_pregrad = turn_by(jnp.stack(sent), (4 - at_x) % 4)
    all_pregrad, all_activ = lax.optimization_barrier((all_pregrad, all_activ))
    all_both = lax.all_gather(both.reshape(384, 1024), "x", axis=0, tiled=False)
    all_both = all_both.reshape(4, 2, 192, 1024)
    down_grad = jnp.einsum("xtf,xtd->fd", all_activ, all_both[:, 0], preferred_element_type=F32)
    up_grad = jnp.einsum("xtd,xtf->df", all_both[:, 1], all_pregrad, preferred_element_type=F32)
    return (input_grad, up_grad, down_grad)


def solution(mesh):
    fine = Mesh(mesh.devices.reshape(4, 2, 4, 4, 4), ("y", "c", "x", "za", "zb"))
    tokens, width = ("x", "za", "zb"), ("y", "c")
    return jax.shard_map(
        local,
        mesh=fine,
        in_specs=(
            P(tokens, width),
            P(tokens, width),
            P(width, tokens),
            P(width, tokens),
            P(tokens, width),
        ),
        out_specs=(P(tokens, width), P(width, tokens), P(tokens, width)),
        check_vma=False,
    )
```

```python
import math

import jax
import jax.numpy as jnp
from jax import lax
from jax.sharding import Mesh, PartitionSpec as P

BF = jnp.bfloat16
F32 = jnp.float32


def gelu_parts(preact):
    value = preact.astype(F32)
    normal_cdf = 0.5 * (1.0 + jax.scipy.special.erf(value / math.sqrt(2.0)))
    density = jnp.exp(-0.5 * value * value) / math.sqrt(2.0 * math.pi)
    return (value * normal_cdf, normal_cdf + value * density)


def exchange(blocks, axis):
    return lax.all_to_all(blocks, axis, split_axis=0, concat_axis=0, tiled=False)


def spread(block, axis, n=4):
    return exchange(jnp.broadcast_to(block[None], (n,) + block.shape), axis)


def halves_down(block):
    lead, (rows, cols) = block.shape[:-2], block.shape[-2:]
    split = block.reshape(*lead, rows, 2, cols // 2)
    return jnp.swapaxes(split, -3, -2).reshape(*lead, rows * 2, cols // 2)


def halves_across(block):
    lead, (rows, cols) = block.shape[:-2], block.shape[-2:]
    split = block.reshape(*lead, 2, rows // 2, cols)
    return jnp.swapaxes(split, -3, -2).reshape(*lead, rows // 2, cols * 2)


def shift(k):
    return [(i, (i + k) % 4) for i in range(4)]


def near_x(block):
    return lax.ppermute(block, "x", shift(1)), lax.ppermute(block, "x", shift(-1))


def far_x(before, after):
    half = before.shape[0] // 2
    return jnp.concatenate(
        [lax.ppermute(before[:half], "x", shift(1)), lax.ppermute(after[half:], "x", shift(-1))]
    )


def turn_by(blocks, start):
    twice = jnp.concatenate([blocks, blocks[:3]])
    return lax.dynamic_slice_in_dim(twice, start, 4, axis=0)


def half_tokens(partial, at_x, half):
    blocks = [
        lax.dynamic_slice(partial, ((at_x + d) % 4, 0, half, 0, 0), (1, 4, 1, 24, 256)) for d in range(4)
    ]
    return jnp.concatenate(blocks).reshape(4, 96, 256)


def local(inputs, out_grad, preact, up_weight, down_weight):
    core, at_x = lax.axis_index("c"), lax.axis_index("x")
    wide_down = lax.all_gather(down_weight, "x", axis=0, tiled=False)

    both = jnp.concatenate([halves_down(out_grad), halves_down(inputs)], axis=0)
    both = spread(both, "za")
    rows_first = preact.reshape(2, 4, 12, 256).transpose(1, 0, 2, 3).reshape(96, 256)
    swap = [(4 * a + b, 4 * ((b - a) % 4) + a) for a in range(4) for b in range(4)]
    turned = lax.ppermute(rows_first, ("y", "x"), swap)
    both, turned = lax.optimization_barrier((both, turned))
    both = halves_across(both.reshape(4, 2, 24, 512)).swapaxes(0, 1).reshape(96, 1024)
    both = spread(both, "zb").reshape(4, 2, 48, 1024).swapaxes(0, 1).reshape(2, 192, 1024)
    grads = both[0]
    before, after = near_x(up_weight)
    grads, before, after = lax.optimization_barrier((grads, before, after))

    partial = jnp.einsum("td,xfd->xtf", grads, wide_down, preferred_element_type=F32)
    partial = partial.reshape(4, 4, 2, 24, 256)
    theirs = lax.ppermute(half_tokens(partial, at_x, 1 - core), "c", [(0, 1), (1, 0)])
    pair = (half_tokens(partial, at_x, core) + theirs).astype(BF)
    activ, _ = gelu_parts(rows_first)
    own = spread(jnp.concatenate([pair, activ.astype(BF)[None], turned[None]]), "y")
    own, far = lax.optimization_barrier((own, far_x(before, after)))
    hidden_grad = own[:, :4].astype(F32).sum(0)
    _, slope = gelu_parts(own[:, 5])
    own = jnp.concatenate([(hidden_grad * slope).astype(BF), own[:, 4]])
    own = lax.all_gather(own, "c", axis=0, tiled=False).reshape(2, 2, 4, 4, 24, 256)
    own = own.transpose(1, 2, 3, 0, 4, 5).reshape(2, 4, 192, 256)
    pregrad, all_activ = own[0], own[1]

    wide_up = jnp.stack([up_weight, after, far, before])
    part = jnp.einsum("xtf,xdf->td", pregrad, wide_up, preferred_element_type=F32)
    part = part.astype(BF).reshape(4, 4, 12, 1024).swapaxes(0, 1)
    part = exchange(halves_down(part.reshape(16, 12, 1024)), ("za", "zb"))
    input_grad = halves_across(part.astype(F32).sum(0)).astype(BF)

    sent = [pregrad[0]] + [lax.ppermute(pregrad[k], "x", shift(k)) for k in (3, 2, 1)]
    all_pregrad = turn_by(jnp.stack(sent), (4 - at_x) % 4)
    all_pregrad, all_activ = lax.optimization_barrier((all_pregrad, all_activ))
    all_both = lax.all_gather(both.reshape(384, 1024), "x", axis=0, tiled=False)
    all_both = all_both.reshape(4, 2, 192, 1024)
    down_grad = jnp.einsum("xtf,xtd->fd", all_activ, all_both[:, 0], preferred_element_type=F32)
    up_grad = jnp.einsum("xtd,xtf->df", all_both[:, 1], all_pregrad, preferred_element_type=F32)
    return (input_grad, up_grad, down_grad)


def solution(mesh):
    fine = Mesh(mesh.devices.reshape(4, 2, 4, 4, 4), ("y", "c", "x", "za", "zb"))
    tokens, width = ("x", "za", "zb"), ("y", "c")
    return jax.shard_map(
        local,
        mesh=fine,
        in_specs=(
            P(tokens, width),
            P(tokens, width),
            P(width, tokens),
            P(width, tokens),
            P(tokens, width),
        ),
        out_specs=(P(tokens, width), P(width, tokens), P(tokens, width)),
        check_vma=False,
    )
```

```python
import math

import jax
import jax.numpy as jnp
from jax import lax
from jax.sharding import Mesh, PartitionSpec as P

BF = jnp.bfloat16
F32 = jnp.float32


def gelu_parts(preact):
    value = preact.astype(F32)
    normal_cdf = 0.5 * (1.0 + jax.scipy.special.erf(value / math.sqrt(2.0)))
    density = jnp.exp(-0.5 * value * value) / math.sqrt(2.0 * math.pi)
    return (value * normal_cdf, normal_cdf + value * density)


def exchange(blocks, axis):
    return lax.all_to_all(blocks, axis, split_axis=0, concat_axis=0, tiled=False)


def spread(block, axis, n=4):
    return exchange(jnp.broadcast_to(block[None], (n,) + block.shape), axis)


def halves_down(block):
    lead, (rows, cols) = block.shape[:-2], block.shape[-2:]
    split = block.reshape(*lead, rows, 2, cols // 2)
    return jnp.swapaxes(split, -3, -2).reshape(*lead, rows * 2, cols // 2)


def halves_across(block):
    lead, (rows, cols) = block.shape[:-2], block.shape[-2:]
    split = block.reshape(*lead, 2, rows // 2, cols)
    return jnp.swapaxes(split, -3, -2).reshape(*lead, rows // 2, cols * 2)


def shift(k):
    return [(i, (i + k) % 4) for i in range(4)]


def near_x(block):
    return lax.ppermute(block, "x", shift(1)), lax.ppermute(block, "x", shift(-1))


def far_x(before, after):
    half = before.shape[0] // 2
    return jnp.concatenate(
        [lax.ppermute(before[:half], "x", shift(1)), lax.ppermute(after[half:], "x", shift(-1))]
    )


def turn_by(blocks, start):
    twice = jnp.concatenate([blocks, blocks[:3]])
    return lax.dynamic_slice_in_dim(twice, start, 4, axis=0)


def half_tokens(partial, at_x, half):
    blocks = [lax.dynamic_slice(partial, ((at_x + d) % 4, half, 0, 0), (1, 1, 96, 256)) for d in range(4)]
    return jnp.concatenate(blocks).reshape(4, 96, 256)


def others_y(block):
    return [lax.ppermute(block, "y", shift(k)) for k in (3, 2, 1)]


def local(inputs, out_grad, preact, up_weight, down_weight):
    core, at_x, at_y = lax.axis_index("c"), lax.axis_index("x"), lax.axis_index("y")
    wide_down = lax.all_gather(down_weight, "x", axis=0, tiled=False)

    grads = spread(halves_down(out_grad), ("za", "zb"), 16)
    swap = [(4 * a + b, 4 * ((b - a) % 4) + a) for a in range(4) for b in range(4)]
    turned = lax.ppermute(preact, ("y", "x"), swap)
    turned = jnp.stack([turned, preact])
    turned = jnp.stack([turned] + others_y(turned))
    before, after = near_x(up_weight)
    grads, turned, before, after = lax.optimization_barrier((grads, turned, before, after))
    grads = halves_across(grads).reshape(192, 1024)
    inputs, grads = lax.optimization_barrier((inputs, grads))
    ins = halves_across(spread(halves_down(inputs), ("za", "zb"), 16)).reshape(192, 1024)
    turned = turn_by(turned, (4 - at_y) % 4)
    _, slope = gelu_parts(turned[:, 0])
    activ, _ = gelu_parts(turned[:, 1])

    partial = jnp.einsum("td,xfd->xtf", grads, wide_down, preferred_element_type=F32)
    partial = partial.reshape(4, 2, 96, 256)
    theirs = lax.ppermute(half_tokens(partial, at_x, 1 - core), "c", [(0, 1), (1, 0)])
    pair = (half_tokens(partial, at_x, core) + theirs).astype(BF)
    sums = others_y(pair)
    far = far_x(before, after)
    pair, sums, far = lax.optimization_barrier((pair, sums, far))
    hidden_grad = sum((s.astype(F32) for s in sums), pair.astype(F32))
    pregrad = lax.all_gather((hidden_grad * slope).astype(BF), "c", axis=1, tiled=False)
    pregrad = pregrad.reshape(4, 192, 256)

    wide_up = jnp.stack([up_weight, after, far, before])
    part = jnp.einsum("xtf,xdf->td", pregrad, wide_up, preferred_element_type=F32)
    part = exchange(halves_down(part.astype(BF).reshape(16, 12, 1024)), ("za", "zb"))
    input_grad = halves_across(part.astype(F32).sum(0)).astype(BF)

    sent = [pregrad[0]] + [lax.ppermute(pregrad[k], "x", shift(k)) for k in (3, 2, 1)]
    all_pregrad = turn_by(jnp.stack(sent), (4 - at_x) % 4)
    all_activ = lax.all_gather(activ.astype(BF), "c", axis=1, tiled=False).reshape(4, 192, 256)
    all_pregrad, all_activ = lax.optimization_barrier((all_pregrad, all_activ))
    all_grads = lax.all_gather(grads, "x", axis=0, tiled=False)
    all_inputs = lax.all_gather(ins, "x", axis=0, tiled=False)
    down_grad = jnp.einsum("xtf,xtd->fd", all_activ, all_grads, preferred_element_type=F32)
    up_grad = jnp.einsum("xtd,xtf->df", all_inputs, all_pregrad, preferred_element_type=F32)
    return (input_grad, up_grad, down_grad)


def solution(mesh):
    fine = Mesh(mesh.devices.reshape(4, 2, 4, 4, 4), ("y", "c", "x", "za", "zb"))
    tokens, width = ("x", "za", "zb"), ("y", "c")
    return jax.shard_map(
        local,
        mesh=fine,
        in_specs=(
            P(tokens, width),
            P(tokens, width),
            P(width, tokens),
            P(width, tokens),
            P(tokens, width),
        ),
        out_specs=(P(tokens, width), P(width, tokens), P(tokens, width)),
        check_vma=False,
    )
```

```python
import math

import jax
import jax.numpy as jnp
from jax import lax
from jax.sharding import Mesh, PartitionSpec as P

BF = jnp.bfloat16
F32 = jnp.float32


def gelu_parts(preact):
    value = preact.astype(F32)
    normal_cdf = 0.5 * (1.0 + jax.scipy.special.erf(value / math.sqrt(2.0)))
    density = jnp.exp(-0.5 * value * value) / math.sqrt(2.0 * math.pi)
    return (value * normal_cdf, normal_cdf + value * density)


def exchange(blocks, axis):
    return lax.all_to_all(blocks, axis, split_axis=0, concat_axis=0, tiled=False)


def spread(block, axis, n=4):
    return exchange(jnp.broadcast_to(block[None], (n,) + block.shape), axis)


def halves_down(block):
    lead, (rows, cols) = block.shape[:-2], block.shape[-2:]
    split = block.reshape(*lead, rows, 2, cols // 2)
    return jnp.swapaxes(split, -3, -2).reshape(*lead, rows * 2, cols // 2)


def halves_across(block):
    lead, (rows, cols) = block.shape[:-2], block.shape[-2:]
    split = block.reshape(*lead, 2, rows // 2, cols)
    return jnp.swapaxes(split, -3, -2).reshape(*lead, rows // 2, cols * 2)


def shift(k):
    return [(i, (i + k) % 4) for i in range(4)]


def near_x(block):
    return lax.ppermute(block, "x", shift(1)), lax.ppermute(block, "x", shift(-1))


def far_x(before, after):
    half = before.shape[0] // 2
    return jnp.concatenate(
        [lax.ppermute(before[:half], "x", shift(1)), lax.ppermute(after[half:], "x", shift(-1))]
    )


def turn_by(blocks, start):
    turned = [lax.dynamic_index_in_dim(blocks, (start + i) % 4, keepdims=True) for i in range(4)]
    return jnp.concatenate(turned)


def local(inputs, out_grad, preact, up_weight, down_weight):
    core, at_x = lax.axis_index("c"), lax.axis_index("x")

    both = jnp.concatenate([halves_down(out_grad), halves_down(inputs)], axis=0)
    both = spread(both, ("za", "zb"), 16)
    swap = [(4 * a + b, 4 * ((b - a) % 4) + a) for a in range(4) for b in range(4)]
    turned = lax.ppermute(preact, ("y", "x"), swap)
    before, after = near_x(down_weight)
    far = far_x(before, after)
    both, turned, before, after, far = lax.optimization_barrier((both, turned, before, after, far))
    wide_down = jnp.stack([down_weight, after, far, before])
    wide_up = lax.all_gather(up_weight, "x", axis=0, tiled=False)
    grads = halves_across(both[:, :24]).reshape(192, 1024)
    ins = halves_across(both[:, 24:]).reshape(192, 1024)

    partial = jnp.einsum("td,xfd->xtf", grads, wide_down, preferred_element_type=F32)
    partial = partial.reshape(4, 2, 96, 256)
    mine = lax.dynamic_index_in_dim(partial, core, axis=1, keepdims=False)
    theirs = lax.dynamic_index_in_dim(partial, 1 - core, axis=1, keepdims=False)
    pair = (mine + lax.ppermute(theirs, "c", [(0, 1), (1, 0)])).astype(BF)
    activ, _ = gelu_parts(preact)
    own = spread(jnp.concatenate([pair, activ.astype(BF)[None], turned[None]]), "y")
    wide_up = turn_by(wide_up, at_x)
    own, wide_up = lax.optimization_barrier((own, wide_up))
    hidden_grad = own[:, :4].astype(F32).sum(0)
    _, slope = gelu_parts(own[:, 5])
    own = jnp.concatenate([(hidden_grad * slope).astype(BF), own[:, 4]])
    own = lax.all_gather(own, "c", axis=1, tiled=False).reshape(2, 4, 192, 256)
    pregrad, all_activ = own[0], own[1]

    part = jnp.einsum("xtf,xdf->td", pregrad, wide_up, preferred_element_type=F32)
    part = exchange(halves_down(part.astype(BF).reshape(16, 12, 1024)), ("za", "zb"))

    sent = [pregrad[0]] + [lax.ppermute(pregrad[k], "x", shift(k)) for k in (3, 2, 1)]
    all_pregrad = turn_by(jnp.stack(sent), 4 - at_x)
    all_pregrad, all_activ = lax.optimization_barrier((all_pregrad, all_activ))
    all_both = lax.all_gather(jnp.concatenate([grads, ins]), "x", axis=0, tiled=False)
    all_both = all_both.reshape(4, 2, 192, 1024)
    down_grad = jnp.einsum("xtf,xtd->fd", all_activ, all_both[:, 0], preferred_element_type=F32)
    up_grad = jnp.einsum("xtd,xtf->df", all_both[:, 1], all_pregrad, preferred_element_type=F32)
    part, up_grad, down_grad = lax.optimization_barrier((part, up_grad, down_grad))
    input_grad = halves_across(part.astype(F32).sum(0)).astype(BF)
    return (input_grad, up_grad, down_grad)


def solution(mesh):
    fine = Mesh(mesh.devices.reshape(4, 2, 4, 4, 4), ("y", "c", "x", "za", "zb"))
    tokens, width = ("x", "za", "zb"), ("y", "c")
    return jax.shard_map(
        local,
        mesh=fine,
        in_specs=(
            P(tokens, width),
            P(tokens, width),
            P(width, tokens),
            P(width, tokens),
            P(tokens, width),
        ),
        out_specs=(P(tokens, width), P(width, tokens), P(tokens, width)),
        check_vma=False,
    )
```

```python
import math

import jax
import jax.numpy as jnp
from jax import lax
from jax.experimental import pallas as pl
from jax.experimental.pallas import tpu as pltpu
from jax.sharding import Mesh, PartitionSpec as P

BF = jnp.bfloat16
F32 = jnp.float32


def gelu_parts(preact):
    value = preact.astype(F32)
    normal_cdf = 0.5 * (1.0 + jax.scipy.special.erf(value / math.sqrt(2.0)))
    density = jnp.exp(-0.5 * value * value) / math.sqrt(2.0 * math.pi)
    return (value * normal_cdf, normal_cdf + value * density)


def exchange(blocks, axis):
    return lax.all_to_all(blocks, axis, split_axis=0, concat_axis=0, tiled=False)


def spread(block, axis, n=4):
    return exchange(jnp.broadcast_to(block[None], (n,) + block.shape), axis)


def call(body, outs, scratch, flops, operands, smem=0):
    moved = sum(a.size * a.dtype.itemsize for a in (*operands, *outs))
    spaces = [pltpu.SMEM] * smem + [pltpu.VMEM] * (len(operands) - smem)
    return pl.pallas_call(
        body,
        out_shape=outs,
        in_specs=[pl.BlockSpec(memory_space=space) for space in spaces],
        out_specs=[pl.BlockSpec(memory_space=pltpu.VMEM)] * len(outs),
        scratch_shapes=[pltpu.VMEM(shape, F32) for shape in scratch],
        cost_estimate=pl.CostEstimate(flops=flops, bytes_accessed=moved, transcendentals=0),
        compiler_params=pltpu.CompilerParams(vmem_limit_bytes=40 * 2**20),
    )(*operands)


def times_transposed(a, b):
    return lax.dot_general(a, b, (((1,), (1,)), ((), ())), preferred_element_type=F32)


def lay_out_kernel(grad_ref, in_ref, out_ref, rows):
    for k, ref in enumerate((grad_ref, in_ref)):
        block = ref[...].astype(F32)
        rows[24 * k : 24 * k + 12] = block[:, :512]
        rows[24 * k + 12 : 24 * k + 24] = block[:, 512:]
    block = rows[...].astype(BF)
    for z in range(16):
        out_ref[z] = block


def hidden_kernel(core_ref, both_ref, own_ref, after_ref, far0_ref, far1_ref, before_ref, *refs):
    mine_ref, theirs_ref, tokens_ref, rows, grads, ins = refs
    for z in range(16):
        rows[z] = both_ref[z].astype(F32)
        here = slice(12 * z, 12 * z + 12)
        grads[here, :512] = rows[z, 0:12]
        grads[here, 512:] = rows[z, 12:24]
        ins[here, :512] = rows[z, 24:36]
        ins[here, 512:] = rows[z, 36:48]
    tokens_ref[0] = grads[...].astype(BF)
    tokens_ref[1] = ins[...].astype(BF)
    first = pl.multiple_of(core_ref[0] * 96, 96)
    second = pl.multiple_of(96 - core_ref[0] * 96, 96)
    for start, out_ref in ((second, theirs_ref), (first, mine_ref)):
        half = grads[pl.ds(start, 96)].astype(BF)
        out_ref[0] = times_transposed(half, own_ref[...])
        out_ref[1] = times_transposed(half, after_ref[...])
        out_ref[2, :, :128] = times_transposed(half, far0_ref[...])
        out_ref[2, :, 128:] = times_transposed(half, far1_ref[...])
        out_ref[3] = times_transposed(half, before_ref[...])


def part_kernel(x_ref, pregrad_ref, up_ref, out_ref, total, rows):
    for d in range(4):
        product = times_transposed(pregrad_ref[d], up_ref[lax.rem(x_ref[0] + d, 4)])
        total[...] = product if d == 0 else total[...] + product
    for z in range(16):
        here = slice(12 * z, 12 * z + 12)
        rows[z, 0:12] = total[here, :512]
        rows[z, 12:24] = total[here, 512:]
        out_ref[z] = rows[z].astype(BF)


def sum_kernel(part_ref, out_ref, rows):
    total = part_ref[0].astype(F32)
    for z in range(1, 16):
        total = total + part_ref[z].astype(F32)
    rows[...] = total
    out_ref[:, :512] = rows[0:12].astype(BF)
    out_ref[:, 512:] = rows[12:24].astype(BF)


def shift(k):
    return [(i, (i + k) % 4) for i in range(4)]


def near_x(block):
    return lax.ppermute(block, "x", shift(1)), lax.ppermute(block, "x", shift(-1))


def far_x(before, after):
    half = before.shape[0] // 2
    return lax.ppermute(before[:half], "x", shift(1)), lax.ppermute(after[half:], "x", shift(-1))


def turn_by(blocks, start):
    turned = [lax.dynamic_index_in_dim(blocks, (start + i) % 4, keepdims=True) for i in range(4)]
    return jnp.concatenate(turned)


def local(inputs, out_grad, preact, up_weight, down_weight):
    core, at_x = lax.axis_index("c"), lax.axis_index("x")

    sixteen = jax.ShapeDtypeStruct((16, 48, 512), BF)
    (both,) = call(lay_out_kernel, [sixteen], [(48, 512)], 0, (out_grad, inputs))
    both = exchange(both, ("za", "zb"))
    swap = [(4 * a + b, 4 * ((b - a) % 4) + a) for a in range(4) for b in range(4)]
    turned = lax.ppermute(preact, ("y", "x"), swap)
    before, after = near_x(down_weight)
    far = far_x(before, after)
    both, turned, before, after, far = lax.optimization_barrier((both, turned, before, after, far))
    wide_up = lax.all_gather(up_weight, "x", axis=0, tiled=False)

    half = jax.ShapeDtypeStruct((4, 96, 256), F32)
    mine, theirs, tokens = call(
        hidden_kernel,
        [half, half, jax.ShapeDtypeStruct((2, 192, 1024), BF)],
        [(16, 48, 512), (192, 1024), (192, 1024)],
        2 * 192 * 1024 * 1024,
        (core[None], both, down_weight, after, *far, before),
        smem=1,
    )
    pair = (mine + lax.ppermute(theirs, "c", [(0, 1), (1, 0)])).astype(BF)
    activ, _ = gelu_parts(preact)
    own = spread(jnp.concatenate([pair, activ.astype(BF)[None], turned[None]]), "y")
    own, wide_up = lax.optimization_barrier((own, wide_up))
    hidden_grad = own[:, :4].astype(F32).sum(0)
    _, slope = gelu_parts(own[:, 5])
    own = jnp.concatenate([(hidden_grad * slope).astype(BF), own[:, 4]])
    own = lax.all_gather(own, "c", axis=1, tiled=False).reshape(8, 192, 256)
    pregrad, all_activ = own[:4], own[4:]

    (part,) = call(
        part_kernel,
        [jax.ShapeDtypeStruct((16, 24, 512), BF)],
        [(192, 1024), (16, 24, 512)],
        2 * 192 * 1024 * 1024,
        (at_x[None], own, wide_up),
        smem=1,
    )
    part = exchange(part, ("za", "zb"))

    sent = [pregrad[0]] + [lax.ppermute(pregrad[k], "x", shift(k)) for k in (3, 2, 1)]
    all_pregrad = turn_by(jnp.stack(sent), 4 - at_x)
    all_pregrad, all_activ = lax.optimization_barrier((all_pregrad, all_activ))
    all_both = lax.all_gather(tokens, "x", axis=0, tiled=False)
    down_grad = jnp.einsum("xtf,xtd->fd", all_activ, all_both[:, 0], preferred_element_type=F32)
    up_grad = jnp.einsum("xtd,xtf->df", all_both[:, 1], all_pregrad, preferred_element_type=F32)
    part, up_grad, down_grad = lax.optimization_barrier((part, up_grad, down_grad))
    (input_grad,) = call(sum_kernel, [jax.ShapeDtypeStruct((12, 1024), BF)], [(24, 512)], 0, (part,))
    return (input_grad, up_grad, down_grad)


def solution(mesh):
    fine = Mesh(mesh.devices.reshape(4, 2, 4, 4, 4), ("y", "c", "x", "za", "zb"))
    tokens, width = ("x", "za", "zb"), ("y", "c")
    return jax.shard_map(
        local,
        mesh=fine,
        in_specs=(
            P(tokens, width),
            P(tokens, width),
            P(width, tokens),
            P(width, tokens),
            P(tokens, width),
        ),
        out_specs=(P(tokens, width), P(width, tokens), P(tokens, width)),
        check_vma=False,
    )
```

```python
import math

import jax
import jax.numpy as jnp
from jax import lax
from jax.experimental import pallas as pl
from jax.experimental.pallas import tpu as pltpu
from jax.sharding import Mesh, PartitionSpec as P

BF = jnp.bfloat16
F32 = jnp.float32


def gelu_parts(preact):
    value = preact.astype(F32)
    normal_cdf = 0.5 * (1.0 + jax.scipy.special.erf(value / math.sqrt(2.0)))
    density = jnp.exp(-0.5 * value * value) / math.sqrt(2.0 * math.pi)
    return (value * normal_cdf, normal_cdf + value * density)


def exchange(blocks, axis):
    return lax.all_to_all(blocks, axis, split_axis=0, concat_axis=0, tiled=False)


def spread(block, axis, n=4):
    return exchange(jnp.broadcast_to(block[None], (n,) + block.shape), axis)


def call(body, outs, scratch, flops, operands, smem=0):
    moved = sum(a.size * a.dtype.itemsize for a in (*operands, *outs))
    spaces = [pltpu.SMEM] * smem + [pltpu.VMEM] * (len(operands) - smem)
    return pl.pallas_call(
        body,
        out_shape=outs,
        in_specs=[pl.BlockSpec(memory_space=space) for space in spaces],
        out_specs=[pl.BlockSpec(memory_space=pltpu.VMEM)] * len(outs),
        scratch_shapes=[pltpu.VMEM(shape, F32) for shape in scratch],
        cost_estimate=pl.CostEstimate(flops=flops, bytes_accessed=moved, transcendentals=0),
        compiler_params=pltpu.CompilerParams(vmem_limit_bytes=40 * 2**20),
    )(*operands)


def times_transposed(a, b):
    return lax.dot_general(a, b, (((1,), (1,)), ((), ())), preferred_element_type=F32)


def lay_out_kernel(grad_ref, in_ref, out_ref, rows):
    for k, ref in enumerate((grad_ref, in_ref)):
        block = ref[...].astype(F32)
        rows[24 * k : 24 * k + 12] = block[:, :512]
        rows[24 * k + 12 : 24 * k + 24] = block[:, 512:]
    block = rows[...].astype(BF)
    for z in range(16):
        out_ref[z] = block


def hidden_kernel(core_ref, both_ref, own_ref, after_ref, far0_ref, far1_ref, before_ref, *refs):
    mine_ref, theirs_ref, tokens_ref, rows, grads, ins = refs
    for z in range(16):
        rows[z] = both_ref[z].astype(F32)
        here = slice(12 * z, 12 * z + 12)
        grads[here, :512] = rows[z, 0:12]
        grads[here, 512:] = rows[z, 12:24]
        ins[here, :512] = rows[z, 24:36]
        ins[here, 512:] = rows[z, 36:48]
    tokens_ref[0] = grads[...].astype(BF)
    tokens_ref[1] = ins[...].astype(BF)
    first = pl.multiple_of(core_ref[0] * 96, 96)
    second = pl.multiple_of(96 - core_ref[0] * 96, 96)
    for start, out_ref in ((second, theirs_ref), (first, mine_ref)):
        half = grads[pl.ds(start, 96)].astype(BF)
        out_ref[0] = times_transposed(half, own_ref[...])
        out_ref[1] = times_transposed(half, after_ref[...])
        out_ref[2, :, :128] = times_transposed(half, far0_ref[...])
        out_ref[2, :, 128:] = times_transposed(half, far1_ref[...])
        out_ref[3] = times_transposed(half, before_ref[...])


def part_kernel(pregrad_ref, own_ref, after_ref, far0_ref, far1_ref, before_ref, out_ref, total, rows):
    total[...] = times_transposed(pregrad_ref[0], own_ref[...])
    total[...] += times_transposed(pregrad_ref[1], after_ref[...])
    total[:, :512] += times_transposed(pregrad_ref[2], far0_ref[...])
    total[:, 512:] += times_transposed(pregrad_ref[2], far1_ref[...])
    total[...] += times_transposed(pregrad_ref[3], before_ref[...])
    for z in range(16):
        here = slice(12 * z, 12 * z + 12)
        rows[z, 0:12] = total[here, :512]
        rows[z, 12:24] = total[here, 512:]
        out_ref[z] = rows[z].astype(BF)


def sum_kernel(part_ref, out_ref, rows):
    total = part_ref[0].astype(F32)
    for z in range(1, 16):
        total = total + part_ref[z].astype(F32)
    rows[...] = total
    out_ref[:, :512] = rows[0:12].astype(BF)
    out_ref[:, 512:] = rows[12:24].astype(BF)


def shift(k):
    return [(i, (i + k) % 4) for i in range(4)]


def near_x(block):
    return lax.ppermute(block, "x", shift(1)), lax.ppermute(block, "x", shift(-1))


def far_x(before, after):
    half = before.shape[0] // 2
    return lax.ppermute(before[:half], "x", shift(1)), lax.ppermute(after[half:], "x", shift(-1))


def turn_by(blocks, start):
    turned = [lax.dynamic_index_in_dim(blocks, (start + i) % 4, keepdims=True) for i in range(4)]
    return jnp.concatenate(turned)


def local(inputs, out_grad, preact, up_weight, down_weight):
    core, at_x = lax.axis_index("c"), lax.axis_index("x")

    sixteen = jax.ShapeDtypeStruct((16, 48, 512), BF)
    (both,) = call(lay_out_kernel, [sixteen], [(48, 512)], 0, (out_grad, inputs))
    both = exchange(both, ("za", "zb"))
    swap = [(4 * a + b, 4 * ((b - a) % 4) + a) for a in range(4) for b in range(4)]
    turned = lax.ppermute(preact, ("y", "x"), swap)
    before, after = near_x(down_weight)
    far = far_x(before, after)
    up_before, up_after = near_x(up_weight)
    both, turned, before, after, far, up_before, up_after = lax.optimization_barrier(
        (both, turned, before, after, far, up_before, up_after)
    )

    half = jax.ShapeDtypeStruct((4, 96, 256), F32)
    mine, theirs, tokens = call(
        hidden_kernel,
        [half, half, jax.ShapeDtypeStruct((2, 192, 1024), BF)],
        [(16, 48, 512), (192, 1024), (192, 1024)],
        2 * 192 * 1024 * 1024,
        (core[None], both, down_weight, after, *far, before),
        smem=1,
    )
    pair = (mine + lax.ppermute(theirs, "c", [(0, 1), (1, 0)])).astype(BF)
    activ, _ = gelu_parts(preact)
    own = spread(jnp.concatenate([pair, activ.astype(BF)[None], turned[None]]), "y")
    up_far = far_x(up_before, up_after)
    tok_before, tok_after = near_x(tokens)
    own, up_far = lax.optimization_barrier((own, up_far))
    hidden_grad = own[:, :4].astype(F32).sum(0)
    _, slope = gelu_parts(own[:, 5])
    own = jnp.concatenate([(hidden_grad * slope).astype(BF), own[:, 4]])
    own = lax.all_gather(own, "c", axis=1, tiled=False).reshape(8, 192, 256)
    pregrad, all_activ = own[:4], own[4:]

    (part,) = call(
        part_kernel,
        [jax.ShapeDtypeStruct((16, 24, 512), BF)],
        [(192, 1024), (16, 24, 512)],
        2 * 192 * 1024 * 1024,
        (own, up_weight, up_after, *up_far, up_before),
    )
    part = exchange(part, ("za", "zb"))

    all_pregrad = jnp.stack([pregrad[0]] + [lax.ppermute(pregrad[k], "x", shift(k)) for k in (3, 2, 1)])
    all_pregrad, tok_before, tok_after = lax.optimization_barrier((all_pregrad, tok_before, tok_after))
    tok_far = jnp.concatenate(far_x(tok_before.reshape(384, 1024), tok_after.reshape(384, 1024)))
    all_tokens = jnp.stack([tokens, tok_after, tok_far.reshape(2, 192, 1024), tok_before])
    all_activ = turn_by(all_activ, at_x)
    all_pregrad, all_activ = lax.optimization_barrier((all_pregrad, all_activ))
    down_grad = jnp.einsum("xtf,xtd->fd", all_activ, all_tokens[:, 0], preferred_element_type=F32)
    up_grad = jnp.einsum("xtd,xtf->df", all_tokens[:, 1], all_pregrad, preferred_element_type=F32)
    part, up_grad, down_grad = lax.optimization_barrier((part, up_grad, down_grad))
    (input_grad,) = call(sum_kernel, [jax.ShapeDtypeStruct((12, 1024), BF)], [(24, 512)], 0, (part,))
    return (input_grad, up_grad, down_grad)


def solution(mesh):
    fine = Mesh(mesh.devices.reshape(4, 2, 4, 4, 4), ("y", "c", "x", "za", "zb"))
    tokens, width = ("x", "za", "zb"), ("y", "c")
    return jax.shard_map(
        local,
        mesh=fine,
        in_specs=(
            P(tokens, width),
            P(tokens, width),
            P(width, tokens),
            P(width, tokens),
            P(tokens, width),
        ),
        out_specs=(P(tokens, width), P(width, tokens), P(tokens, width)),
        check_vma=False,
    )
```

```python
import math

import jax
import jax.numpy as jnp
from jax import lax
from jax.experimental import pallas as pl
from jax.experimental.pallas import tpu as pltpu
from jax.sharding import Mesh, PartitionSpec as P

BF = jnp.bfloat16
F32 = jnp.float32


def gelu_parts(preact):
    value = preact.astype(F32)
    normal_cdf = 0.5 * (1.0 + jax.scipy.special.erf(value / math.sqrt(2.0)))
    density = jnp.exp(-0.5 * value * value) / math.sqrt(2.0 * math.pi)
    return (value * normal_cdf, normal_cdf + value * density)


def exchange(blocks, axis):
    return lax.all_to_all(blocks, axis, split_axis=0, concat_axis=0, tiled=False)


def spread(block, axis, n=4):
    return exchange(jnp.broadcast_to(block[None], (n,) + block.shape), axis)


def call(body, outs, scratch, flops, operands, smem=0):
    moved = sum(a.size * a.dtype.itemsize for a in (*operands, *outs))
    spaces = [pltpu.SMEM] * smem + [pltpu.VMEM] * (len(operands) - smem)
    return pl.pallas_call(
        body,
        out_shape=outs,
        in_specs=[pl.BlockSpec(memory_space=space) for space in spaces],
        out_specs=[pl.BlockSpec(memory_space=pltpu.VMEM)] * len(outs),
        scratch_shapes=[pltpu.VMEM(shape, F32) for shape in scratch],
        cost_estimate=pl.CostEstimate(flops=flops, bytes_accessed=moved, transcendentals=0),
        compiler_params=pltpu.CompilerParams(vmem_limit_bytes=40 * 2**20),
    )(*operands)


def times_transposed(a, b):
    return lax.dot_general(a, b, (((1,), (1,)), ((), ())), preferred_element_type=F32)


def lay_out_kernel(grad_ref, in_ref, out_ref, rows):
    for k, ref in enumerate((grad_ref, in_ref)):
        block = ref[...].astype(F32)
        rows[24 * k : 24 * k + 12] = block[:, :512]
        rows[24 * k + 12 : 24 * k + 24] = block[:, 512:]
    block = rows[...].astype(BF)
    for z in range(16):
        out_ref[z] = block


def hidden_kernel(core_ref, both_ref, own_ref, after_ref, far0_ref, far1_ref, before_ref, *refs):
    mine_ref, theirs_ref, tokens_ref, rows, grads, ins = refs
    for z in range(16):
        rows[z] = both_ref[z].astype(F32)
        here = slice(12 * z, 12 * z + 12)
        grads[here, :512] = rows[z, 0:12]
        grads[here, 512:] = rows[z, 12:24]
        ins[here, :512] = rows[z, 24:36]
        ins[here, 512:] = rows[z, 36:48]
    tokens_ref[0] = grads[...].astype(BF)
    tokens_ref[1] = ins[...].astype(BF)
    first = pl.multiple_of(core_ref[0] * 96, 96)
    second = pl.multiple_of(96 - core_ref[0] * 96, 96)
    for start, out_ref in ((second, theirs_ref), (first, mine_ref)):
        half = grads[pl.ds(start, 96)].astype(BF)
        out_ref[0] = times_transposed(half, own_ref[...])
        out_ref[1] = times_transposed(half, after_ref[...])
        out_ref[2, :, :128] = times_transposed(half, far0_ref[...])
        out_ref[2, :, 128:] = times_transposed(half, far1_ref[...])
        out_ref[3] = times_transposed(half, before_ref[...])


def part_kernel(pregrad_ref, own_ref, after_ref, far0_ref, far1_ref, before_ref, out_ref, total, rows):
    total[...] = times_transposed(pregrad_ref[0], own_ref[...])
    total[...] += times_transposed(pregrad_ref[1], after_ref[...])
    total[:, :512] += times_transposed(pregrad_ref[2], far0_ref[...])
    total[:, 512:] += times_transposed(pregrad_ref[2], far1_ref[...])
    total[...] += times_transposed(pregrad_ref[3], before_ref[...])
    for z in range(16):
        here = slice(12 * z, 12 * z + 12)
        rows[z, 0:12] = total[here, :512]
        rows[z, 12:24] = total[here, 512:]
        out_ref[z] = rows[z].astype(BF)


def pack_kernel(before_ref, after_ref, own_ref, plus_ref, minus_ref):
    plus_ref[:, :1024] = before_ref[0]
    plus_ref[:, 1024:] = own_ref[1]
    minus_ref[:, :1024] = after_ref[1]
    minus_ref[:, 1024:] = own_ref[3]


def times_tokens(a, b):
    return lax.dot_general(a, b, (((0,), (0,)), ((), ())), preferred_element_type=F32)


def weights_kernel(x_ref, tokens_ref, after_ref, plus_ref, minus_ref, before_ref, own_ref, two_ref, *outs):
    up_ref, down_ref = outs
    up_ref[...] = times_tokens(tokens_ref[1], own_ref[0])
    up_ref[...] += times_tokens(after_ref[1], minus_ref[:, 1024:])
    up_ref[...] += times_tokens(minus_ref[:, :1024], two_ref[...])
    up_ref[...] += times_tokens(before_ref[1], plus_ref[:, 1024:])

    def activ(d):
        return own_ref[4 + lax.rem(x_ref[0] + d, 4)]

    down_ref[...] = times_tokens(activ(0), tokens_ref[0])
    down_ref[...] += times_tokens(activ(1), after_ref[0])
    down_ref[...] += times_tokens(activ(2), plus_ref[:, :1024])
    down_ref[...] += times_tokens(activ(3), before_ref[0])


def sum_kernel(part_ref, out_ref, rows):
    total = part_ref[0].astype(F32)
    for z in range(1, 16):
        total = total + part_ref[z].astype(F32)
    rows[...] = total
    out_ref[:, :512] = rows[0:12].astype(BF)
    out_ref[:, 512:] = rows[12:24].astype(BF)


def shift(k):
    return [(i, (i + k) % 4) for i in range(4)]


def near_x(block):
    return lax.ppermute(block, "x", shift(1)), lax.ppermute(block, "x", shift(-1))


def far_x(before, after):
    half = before.shape[0] // 2
    return lax.ppermute(before[:half], "x", shift(1)), lax.ppermute(after[half:], "x", shift(-1))


def local(inputs, out_grad, preact, up_weight, down_weight):
    core, at_x = lax.axis_index("c"), lax.axis_index("x")

    sixteen = jax.ShapeDtypeStruct((16, 48, 512), BF)
    (both,) = call(lay_out_kernel, [sixteen], [(48, 512)], 0, (out_grad, inputs))
    both = exchange(both, ("za", "zb"))
    swap = [(4 * a + b, 4 * ((b - a) % 4) + a) for a in range(4) for b in range(4)]
    turned = lax.ppermute(preact, ("y", "x"), swap)
    before, after = near_x(down_weight)
    far = far_x(before, after)
    up_before, up_after = near_x(up_weight)
    both, turned, before, after, far, up_before, up_after = lax.optimization_barrier(
        (both, turned, before, after, far, up_before, up_after)
    )

    half = jax.ShapeDtypeStruct((4, 96, 256), F32)
    mine, theirs, tokens = call(
        hidden_kernel,
        [half, half, jax.ShapeDtypeStruct((2, 192, 1024), BF)],
        [(16, 48, 512), (192, 1024), (192, 1024)],
        2 * 192 * 1024 * 1024,
        (core[None], both, down_weight, after, *far, before),
        smem=1,
    )
    pair = (mine + lax.ppermute(theirs, "c", [(0, 1), (1, 0)])).astype(BF)
    activ, _ = gelu_parts(preact)
    own = spread(jnp.concatenate([pair, activ.astype(BF)[None], turned[None]]), "y")
    up_far = far_x(up_before, up_after)
    tok_before, tok_after = near_x(tokens)
    own, up_far = lax.optimization_barrier((own, up_far))
    hidden_grad = sum((own[k, :4].astype(F32) for k in range(1, 4)), own[0, :4].astype(F32))
    _, slope = gelu_parts(own[:, 5])
    own = jnp.concatenate([(hidden_grad * slope).astype(BF), own[:, 4]])
    own = lax.all_gather(own, "c", axis=1, tiled=False).reshape(8, 192, 256)

    (part,) = call(
        part_kernel,
        [jax.ShapeDtypeStruct((16, 24, 512), BF)],
        [(192, 1024), (16, 24, 512)],
        2 * 192 * 1024 * 1024,
        (own, up_weight, up_after, *up_far, up_before),
    )
    part, tok_before, tok_after = lax.optimization_barrier((part, tok_before, tok_after))
    part = exchange(part, ("za", "zb"))

    packed = jax.ShapeDtypeStruct((192, 1280), BF)
    plus, minus = call(pack_kernel, [packed, packed], [], 0, (tok_before, tok_after, own))
    plus, minus = lax.ppermute(plus, "x", shift(1)), lax.ppermute(minus, "x", shift(-1))
    two = lax.ppermute(own[2], "x", shift(2))
    up_grad, down_grad = call(
        weights_kernel,
        [jax.ShapeDtypeStruct((1024, 256), F32), jax.ShapeDtypeStruct((256, 1024), F32)],
        [],
        4 * 768 * 1024 * 256,
        (at_x[None], tokens, tok_after, plus, minus, tok_before, own, two),
        smem=1,
    )
    part, up_grad, down_grad = lax.optimization_barrier((part, up_grad, down_grad))
    (input_grad,) = call(sum_kernel, [jax.ShapeDtypeStruct((12, 1024), BF)], [(24, 512)], 0, (part,))
    return (input_grad, up_grad, down_grad)


def solution(mesh):
    fine = Mesh(mesh.devices.reshape(4, 2, 4, 4, 4), ("y", "c", "x", "za", "zb"))
    tokens, width = ("x", "za", "zb"), ("y", "c")
    return jax.shard_map(
        local,
        mesh=fine,
        in_specs=(
            P(tokens, width),
            P(tokens, width),
            P(width, tokens),
            P(width, tokens),
            P(tokens, width),
        ),
        out_specs=(P(tokens, width), P(width, tokens), P(tokens, width)),
        check_vma=False,
    )
```

```python
import math

import jax
import jax.numpy as jnp
from jax import lax
from jax.experimental import pallas as pl
from jax.experimental.pallas import tpu as pltpu
from jax.sharding import Mesh, PartitionSpec as P

BF = jnp.bfloat16
F32 = jnp.float32


def gelu_parts(preact):
    value = preact.astype(F32)
    normal_cdf = 0.5 * (1.0 + jax.scipy.special.erf(value / math.sqrt(2.0)))
    density = jnp.exp(-0.5 * value * value) / math.sqrt(2.0 * math.pi)
    return (value * normal_cdf, normal_cdf + value * density)


def exchange(blocks, axis):
    return lax.all_to_all(blocks, axis, split_axis=0, concat_axis=0, tiled=False)


def spread(block, axis, n=4):
    return exchange(jnp.broadcast_to(block[None], (n,) + block.shape), axis)


def call(body, outs, scratch, flops, operands, smem=0, moved=None):
    if moved is None:
        moved = sum(a.size * a.dtype.itemsize for a in (*operands, *outs))
    spaces = [pltpu.SMEM] * smem + [pltpu.VMEM] * (len(operands) - smem)
    return pl.pallas_call(
        body,
        out_shape=outs,
        in_specs=[pl.BlockSpec(memory_space=space) for space in spaces],
        out_specs=[pl.BlockSpec(memory_space=pltpu.VMEM)] * len(outs),
        scratch_shapes=[pltpu.VMEM(shape, F32) for shape in scratch],
        cost_estimate=pl.CostEstimate(flops=flops, bytes_accessed=moved, transcendentals=0),
        compiler_params=pltpu.CompilerParams(vmem_limit_bytes=40 * 2**20),
    )(*operands)


def times_transposed(a, b):
    return lax.dot_general(a, b, (((1,), (1,)), ((), ())), preferred_element_type=F32)


def lay_out_kernel(grad_ref, in_ref, out_ref, rows):
    for k, ref in enumerate((grad_ref, in_ref)):
        block = ref[...].astype(F32)
        rows[24 * k : 24 * k + 12] = block[:, :512]
        rows[24 * k + 12 : 24 * k + 24] = block[:, 512:]
    block = rows[...].astype(BF)
    for z in range(16):
        out_ref[z] = block


def hidden_kernel(core_ref, both_ref, own_ref, after_ref, far0_ref, far1_ref, before_ref, *refs):
    mine_ref, theirs_ref, tokens_ref, rows, grads, ins = refs
    for z in range(16):
        rows[z] = both_ref[z].astype(F32)
        here = slice(12 * z, 12 * z + 12)
        grads[here, :512] = rows[z, 0:12]
        grads[here, 512:] = rows[z, 12:24]
        ins[here, :512] = rows[z, 24:36]
        ins[here, 512:] = rows[z, 36:48]
    tokens_ref[0] = grads[...].astype(BF)
    tokens_ref[1] = ins[...].astype(BF)
    first = pl.multiple_of(core_ref[0] * 96, 96)
    second = pl.multiple_of(96 - core_ref[0] * 96, 96)
    for start, out_ref in ((second, theirs_ref), (first, mine_ref)):
        half = grads[pl.ds(start, 96)].astype(BF)
        out_ref[0] = times_transposed(half, own_ref[...])
        out_ref[1] = times_transposed(half, after_ref[...])
        out_ref[2, :, :128] = times_transposed(half, far0_ref[...])
        out_ref[2, :, 128:] = times_transposed(half, far1_ref[...])
        out_ref[3] = times_transposed(half, before_ref[...])


def part_kernel(pregrad_ref, own_ref, after_ref, far0_ref, far1_ref, before_ref, out_ref, total, rows):
    total[...] = times_transposed(pregrad_ref[0], own_ref[...])
    total[...] += times_transposed(pregrad_ref[1], after_ref[...])
    total[:, :512] += times_transposed(pregrad_ref[2], far0_ref[...])
    total[:, 512:] += times_transposed(pregrad_ref[2], far1_ref[...])
    total[...] += times_transposed(pregrad_ref[3], before_ref[...])
    for z in range(16):
        here = slice(12 * z, 12 * z + 12)
        rows[z, 0:12] = total[here, :512]
        rows[z, 12:24] = total[here, 512:]
        out_ref[z] = rows[z].astype(BF)


def pack_kernel(before_ref, after_ref, own_ref, plus_ref, minus_ref):
    plus_ref[:, :1024] = before_ref[0]
    plus_ref[:, 1024:] = own_ref[1]
    minus_ref[:, :1024] = after_ref[1]
    minus_ref[:, 1024:] = own_ref[3]


def times_tokens(a, b):
    return lax.dot_general(a, b, (((0,), (0,)), ((), ())), preferred_element_type=F32)


def weights_kernel(x_ref, tokens_ref, after_ref, plus_ref, minus_ref, before_ref, own_ref, two_ref, *outs):
    up_ref, down_ref = outs
    up_ref[...] = times_tokens(tokens_ref[1], own_ref[0])
    up_ref[...] += times_tokens(after_ref[1], minus_ref[:, 1024:])
    up_ref[...] += times_tokens(minus_ref[:, :1024], two_ref[...])
    up_ref[...] += times_tokens(before_ref[1], plus_ref[:, 1024:])

    def activ(d):
        return own_ref[4 + lax.rem(x_ref[0] + d, 4)]

    down_ref[...] = times_tokens(activ(0), tokens_ref[0])
    down_ref[...] += times_tokens(activ(1), after_ref[0])
    down_ref[...] += times_tokens(activ(2), plus_ref[:, :1024])
    down_ref[...] += times_tokens(activ(3), before_ref[0])


def sum_kernel(part_ref, out_ref, rows):
    total = part_ref[0].astype(F32)
    for z in range(1, 16):
        total = total + part_ref[z].astype(F32)
    rows[...] = total
    out_ref[:, :512] = rows[0:12].astype(BF)
    out_ref[:, 512:] = rows[12:24].astype(BF)


def shift(k):
    return [(i, (i + k) % 4) for i in range(4)]


def near_x(block):
    return lax.ppermute(block, "x", shift(1)), lax.ppermute(block, "x", shift(-1))


def far_x(before, after):
    half = before.shape[0] // 2
    return lax.ppermute(before[:half], "x", shift(1)), lax.ppermute(after[half:], "x", shift(-1))


def local(inputs, out_grad, preact, up_weight, down_weight):
    core, at_x = lax.axis_index("c"), lax.axis_index("x")

    sixteen = jax.ShapeDtypeStruct((16, 48, 512), BF)
    (both,) = call(lay_out_kernel, [sixteen], [(48, 512)], 0, (out_grad, inputs))
    both = exchange(both, ("za", "zb"))
    swap = [(4 * a + b, 4 * ((b - a) % 4) + a) for a in range(4) for b in range(4)]
    turned = lax.ppermute(preact, ("y", "x"), swap)
    before, after = near_x(down_weight)
    far = far_x(before, after)
    up_before, up_after = near_x(up_weight)
    turned, far_before, far_after = lax.optimization_barrier((turned, up_before, up_after))
    up_far = far_x(far_before, far_after)
    both, before, after, far, up_before, up_after = lax.optimization_barrier(
        (both, before, after, far, up_before, up_after)
    )

    half = jax.ShapeDtypeStruct((4, 96, 256), F32)
    mine, theirs, tokens = call(
        hidden_kernel,
        [half, half, jax.ShapeDtypeStruct((2, 192, 1024), BF)],
        [(16, 48, 512), (192, 1024), (192, 1024)],
        2 * 192 * 1024 * 1024,
        (core[None], both, down_weight, after, *far, before),
        smem=1,
    )
    theirs, up_far = lax.optimization_barrier((theirs, up_far))
    pair = (mine + lax.ppermute(theirs, "c", [(0, 1), (1, 0)])).astype(BF)
    activ, _ = gelu_parts(preact)
    own = spread(jnp.concatenate([pair, activ.astype(BF)[None], turned[None]]), "y")
    tok_before, tok_after = near_x(tokens)
    hidden_grad = sum((own[k, :4].astype(F32) for k in range(1, 4)), own[0, :4].astype(F32))
    _, slope = gelu_parts(own[:, 5])
    own = jnp.concatenate([(hidden_grad * slope).astype(BF), own[:, 4]])
    own = lax.all_gather(own, "c", axis=1, tiled=False).reshape(8, 192, 256)

    (part,) = call(
        part_kernel,
        [jax.ShapeDtypeStruct((16, 24, 512), BF)],
        [(192, 1024), (16, 24, 512)],
        2 * 192 * 1024 * 1024,
        (own, up_weight, up_after, *up_far, up_before),
    )
    _, tok_before, tok_after = lax.optimization_barrier((part, tok_before, tok_after))
    part = exchange(part, ("za", "zb"))

    packed = jax.ShapeDtypeStruct((192, 1280), BF)
    plus, minus = call(pack_kernel, [packed, packed], [], 0, (tok_before, tok_after, own))
    plus, minus = lax.ppermute(plus, "x", shift(1)), lax.ppermute(minus, "x", shift(-1))
    two = lax.ppermute(own[2], "x", shift(2))
    up_grad, down_grad = call(
        weights_kernel,
        [jax.ShapeDtypeStruct((1024, 256), F32), jax.ShapeDtypeStruct((256, 1024), F32)],
        [],
        8 * 4 * 768 * 1024 * 256,
        (at_x[None], tokens, tok_after, plus, minus, tok_before, own, two),
        smem=1,
    )
    part, up_grad, down_grad = lax.optimization_barrier((part, up_grad, down_grad))
    (input_grad,) = call(sum_kernel, [jax.ShapeDtypeStruct((12, 1024), BF)], [(24, 512)], 0, (part,))
    return (input_grad, up_grad, down_grad)


def solution(mesh):
    fine = Mesh(mesh.devices.reshape(4, 2, 4, 4, 4), ("y", "c", "x", "za", "zb"))
    tokens, width = ("x", "za", "zb"), ("y", "c")
    return jax.shard_map(
        local,
        mesh=fine,
        in_specs=(
            P(tokens, width),
            P(tokens, width),
            P(width, tokens),
            P(width, tokens),
            P(tokens, width),
        ),
        out_specs=(P(tokens, width), P(width, tokens), P(tokens, width)),
        check_vma=False,
    )
```

```python
import math

import jax
import jax.numpy as jnp
from jax import lax
from jax.experimental import pallas as pl
from jax.experimental.pallas import tpu as pltpu
from jax.sharding import Mesh, PartitionSpec as P

BF = jnp.bfloat16
F32 = jnp.float32


def gelu_parts(preact):
    value = preact.astype(F32)
    normal_cdf = 0.5 * (1.0 + jax.scipy.special.erf(value / math.sqrt(2.0)))
    density = jnp.exp(-0.5 * value * value) / math.sqrt(2.0 * math.pi)
    return (value * normal_cdf, normal_cdf + value * density)


def exchange(blocks, axis):
    return lax.all_to_all(blocks, axis, split_axis=0, concat_axis=0, tiled=False)


def call(body, outs, scratch, flops, operands, smem=0, moved=None):
    if moved is None:
        moved = sum(a.size * a.dtype.itemsize for a in (*operands, *outs))
    spaces = [pltpu.SMEM] * smem + [pltpu.VMEM] * (len(operands) - smem)
    return pl.pallas_call(
        body,
        out_shape=outs,
        in_specs=[pl.BlockSpec(memory_space=space) for space in spaces],
        out_specs=[pl.BlockSpec(memory_space=pltpu.VMEM)] * len(outs),
        scratch_shapes=[pltpu.VMEM(shape, F32) for shape in scratch],
        cost_estimate=pl.CostEstimate(flops=flops, bytes_accessed=moved, transcendentals=0),
        compiler_params=pltpu.CompilerParams(vmem_limit_bytes=40 * 2**20),
    )(*operands)


def times_transposed(a, b):
    return lax.dot_general(a, b, (((1,), (1,)), ((), ())), preferred_element_type=F32)


def lay_out_kernel(grad_ref, in_ref, out_ref, rows):
    for k, ref in enumerate((grad_ref, in_ref)):
        block = ref[...].astype(F32)
        rows[24 * k : 24 * k + 12] = block[:, :512]
        rows[24 * k + 12 : 24 * k + 24] = block[:, 512:]
    block = rows[...].astype(BF)
    for z in range(16):
        out_ref[z] = block


def hidden_kernel(core_ref, both_ref, own_ref, after_ref, far0_ref, far1_ref, before_ref, *refs):
    mine_ref, theirs_ref, tokens_ref, rows, grads, ins = refs
    for z in range(16):
        rows[z] = both_ref[z].astype(F32)
        here = slice(12 * z, 12 * z + 12)
        grads[here, :512] = rows[z, 0:12]
        grads[here, 512:] = rows[z, 12:24]
        ins[here, :512] = rows[z, 24:36]
        ins[here, 512:] = rows[z, 36:48]
    tokens_ref[0] = grads[...].astype(BF)
    tokens_ref[1] = ins[...].astype(BF)
    first = pl.multiple_of(core_ref[0] * 96, 96)
    second = pl.multiple_of(96 - core_ref[0] * 96, 96)
    for start, out_ref in ((second, theirs_ref), (first, mine_ref)):
        half = grads[pl.ds(start, 96)].astype(BF)
        out_ref[0] = times_transposed(half, own_ref[...])
        out_ref[1] = times_transposed(half, after_ref[...])
        out_ref[2, :, :128] = times_transposed(half, far0_ref[...])
        out_ref[2, :, 128:] = times_transposed(half, far1_ref[...])
        out_ref[3] = times_transposed(half, before_ref[...])


def payload_kernel(mine_ref, theirs_ref, activ_ref, preact_ref, out_ref):
    for k in range(6):
        if k < 4:
            block = (mine_ref[k] + theirs_ref[k]).astype(BF)
        else:
            block = activ_ref[...] if k == 4 else preact_ref[...]
        for y in range(4):
            out_ref[y, k] = block


def slope_kernel(own_ref, out_ref):
    for d in range(4):
        hidden = own_ref[0, d].astype(F32)
        for y in range(1, 4):
            hidden = hidden + own_ref[y, d].astype(F32)
        _, slope = gelu_parts(own_ref[d, 5])
        out_ref[d] = (hidden * slope).astype(BF)
        out_ref[4 + d] = own_ref[d, 4]


def part_kernel(pregrad_ref, own_ref, after_ref, far0_ref, far1_ref, before_ref, out_ref, total, rows):
    total[...] = times_transposed(pregrad_ref[0], own_ref[...])
    total[...] += times_transposed(pregrad_ref[1], after_ref[...])
    total[:, :512] += times_transposed(pregrad_ref[2], far0_ref[...])
    total[:, 512:] += times_transposed(pregrad_ref[2], far1_ref[...])
    total[...] += times_transposed(pregrad_ref[3], before_ref[...])
    for z in range(16):
        here = slice(12 * z, 12 * z + 12)
        rows[z, 0:12] = total[here, :512]
        rows[z, 12:24] = total[here, 512:]
        out_ref[z] = rows[z].astype(BF)


def times_tokens(a, b):
    return lax.dot_general(a, b, (((0,), (0,)), ((), ())), preferred_element_type=F32)


def weights_kernel(x_ref, own_ref, *refs):
    tokens, pregrad, (up_ref, down_ref) = refs[:4], (own_ref.at[0], *refs[4:7]), refs[7:]
    for d in range(4):
        up = times_tokens(tokens[d][1], pregrad[d][...])
        down = times_tokens(own_ref[4 + lax.rem(x_ref[0] + d, 4)], tokens[d][0])
        up_ref[...] = up if d == 0 else up_ref[...] + up
        down_ref[...] = down if d == 0 else down_ref[...] + down


def sum_kernel(part_ref, out_ref, rows):
    total = part_ref[0].astype(F32)
    for z in range(1, 16):
        total = total + part_ref[z].astype(F32)
    rows[...] = total
    out_ref[:, :512] = rows[0:12].astype(BF)
    out_ref[:, 512:] = rows[12:24].astype(BF)


def shift(k):
    return [(i, (i + k) % 4) for i in range(4)]


def near_x(block):
    return lax.ppermute(block, "x", shift(1)), lax.ppermute(block, "x", shift(-1))


def far_x(before, after):
    half = before.shape[0] // 2
    return lax.ppermute(before[:half], "x", shift(1)), lax.ppermute(after[half:], "x", shift(-1))


def local(inputs, out_grad, preact, up_weight, down_weight):
    core, at_x = lax.axis_index("c"), lax.axis_index("x")

    sixteen = jax.ShapeDtypeStruct((16, 48, 512), BF)
    (both,) = call(lay_out_kernel, [sixteen], [(48, 512)], 0, (out_grad, inputs))
    both = exchange(both, ("za", "zb"))
    swap = [(4 * a + b, 4 * ((b - a) % 4) + a) for a in range(4) for b in range(4)]
    turned = lax.ppermute(preact, ("y", "x"), swap)
    before, after = near_x(down_weight)
    far = far_x(before, after)
    up_before, up_after = near_x(up_weight)
    up_far = far_x(up_before, up_after)
    both, before, after, far, up_before, up_after = lax.optimization_barrier(
        (both, before, after, far, up_before, up_after)
    )

    half = jax.ShapeDtypeStruct((4, 96, 256), F32)
    mine, theirs, tokens = call(
        hidden_kernel,
        [half, half, jax.ShapeDtypeStruct((2, 192, 1024), BF)],
        [(16, 48, 512), (192, 1024), (192, 1024)],
        2 * 192 * 1024 * 1024,
        (core[None], both, down_weight, after, *far, before),
        smem=1,
    )
    theirs, turned, up_far = lax.optimization_barrier((theirs, turned, up_far))
    theirs = lax.ppermute(theirs, "c", [(0, 1), (1, 0)])
    activ = gelu_parts(preact)[0].astype(BF)
    (own,) = call(payload_kernel, [jax.ShapeDtypeStruct((4, 6, 96, 256), BF)], [], 0, (mine, theirs, activ, turned))
    own = exchange(own, "y")
    (own,) = call(slope_kernel, [jax.ShapeDtypeStruct((8, 96, 256), BF)], [], 0, (own,))
    own = lax.all_gather(own, "c", axis=1, tiled=False).reshape(8, 192, 256)

    (part,) = call(
        part_kernel,
        [jax.ShapeDtypeStruct((16, 24, 512), BF)],
        [(192, 1024), (16, 24, 512)],
        2 * 192 * 1024 * 1024,
        (own, up_weight, up_after, *up_far, up_before),
    )
    part = exchange(part, ("za", "zb"))

    all_tokens = [tokens] + [lax.ppermute(tokens, "x", shift(k)) for k in (3, 2, 1)]
    all_pregrad = [lax.ppermute(own[k], "x", shift(k)) for k in (3, 2, 1)]
    up_grad, down_grad = call(
        weights_kernel,
        [jax.ShapeDtypeStruct((1024, 256), F32), jax.ShapeDtypeStruct((256, 1024), F32)],
        [],
        16 * 4 * 768 * 1024 * 256,
        (at_x[None], own, *all_tokens, *all_pregrad),
        smem=1,
    )
    part, up_grad, down_grad = lax.optimization_barrier((part, up_grad, down_grad))
    (input_grad,) = call(sum_kernel, [jax.ShapeDtypeStruct((12, 1024), BF)], [(24, 512)], 0, (part,))
    return (input_grad, up_grad, down_grad)


def solution(mesh):
    fine = Mesh(mesh.devices.reshape(4, 2, 4, 4, 4), ("y", "c", "x", "za", "zb"))
    tokens, width = ("x", "za", "zb"), ("y", "c")
    return jax.shard_map(
        local,
        mesh=fine,
        in_specs=(
            P(tokens, width),
            P(tokens, width),
            P(width, tokens),
            P(width, tokens),
            P(tokens, width),
        ),
        out_specs=(P(tokens, width), P(width, tokens), P(tokens, width)),
        check_vma=False,
    )
```

```python
import math

import jax
import jax.numpy as jnp
from jax import lax
from jax.experimental import pallas as pl
from jax.experimental.pallas import tpu as pltpu
from jax.sharding import Mesh, PartitionSpec as P

BF = jnp.bfloat16
F32 = jnp.float32


def gelu_parts(preact):
    value = preact.astype(F32)
    normal_cdf = 0.5 * (1.0 + jax.scipy.special.erf(value / math.sqrt(2.0)))
    density = jnp.exp(-0.5 * value * value) / math.sqrt(2.0 * math.pi)
    return (value * normal_cdf, normal_cdf + value * density)


def exchange(blocks, axis):
    return lax.all_to_all(blocks, axis, split_axis=0, concat_axis=0, tiled=False)


def call(body, outs, scratch, flops, operands, smem=0):
    moved = sum(a.size * a.dtype.itemsize for a in (*operands, *outs))
    spaces = [pltpu.SMEM] * smem + [pltpu.VMEM] * (len(operands) - smem)
    return pl.pallas_call(
        body,
        out_shape=outs,
        in_specs=[pl.BlockSpec(memory_space=space) for space in spaces],
        out_specs=[pl.BlockSpec(memory_space=pltpu.VMEM)] * len(outs),
        scratch_shapes=[pltpu.VMEM(shape, F32) for shape in scratch],
        cost_estimate=pl.CostEstimate(flops=flops, bytes_accessed=moved, transcendentals=0),
        compiler_params=pltpu.CompilerParams(vmem_limit_bytes=16 * 2**20),
    )(*operands)


def times_transposed(a, b):
    return lax.dot_general(a, b, (((1,), (1,)), ((), ())), preferred_element_type=F32)


def lay_out_kernel(grad_ref, in_ref, out_ref, rows):
    for k, ref in enumerate((grad_ref, in_ref)):
        block = ref[...].astype(F32)
        rows[24 * k : 24 * k + 12] = block[:, :512]
        rows[24 * k + 12 : 24 * k + 24] = block[:, 512:]
    block = rows[...].astype(BF)
    for z in range(16):
        out_ref[z] = block


def hidden_kernel(core_ref, both_ref, own_ref, after_ref, far0_ref, far1_ref, before_ref, *refs):
    mine_ref, theirs_ref, tokens_ref, rows, grads, ins = refs
    for z in range(16):
        rows[z] = both_ref[z].astype(F32)
        here = slice(12 * z, 12 * z + 12)
        grads[here, :512] = rows[z, 0:12]
        grads[here, 512:] = rows[z, 12:24]
        ins[here, :512] = rows[z, 24:36]
        ins[here, 512:] = rows[z, 36:48]
    tokens_ref[0] = grads[...].astype(BF)
    tokens_ref[1] = ins[...].astype(BF)
    first = pl.multiple_of(core_ref[0] * 96, 96)
    second = pl.multiple_of(96 - core_ref[0] * 96, 96)
    for start, out_ref in ((second, theirs_ref), (first, mine_ref)):
        half = grads[pl.ds(start, 96)].astype(BF)
        out_ref[0] = times_transposed(half, own_ref[...])
        out_ref[1] = times_transposed(half, after_ref[...])
        out_ref[2, :, :128] = times_transposed(half, far0_ref[...])
        out_ref[2, :, 128:] = times_transposed(half, far1_ref[...])
        out_ref[3] = times_transposed(half, before_ref[...])


def payload_kernel(mine_ref, theirs_ref, preact_ref, turned_ref, out_ref):
    for k in range(6):
        if k < 4:
            block = (mine_ref[k] + theirs_ref[k]).astype(BF)
        else:
            block = gelu_parts(preact_ref[...])[0].astype(BF) if k == 4 else turned_ref[...]
        for y in range(4):
            out_ref[y, k] = block


def slope_kernel(own_ref, out_ref):
    for d in range(4):
        hidden = own_ref[0, d].astype(F32)
        for y in range(1, 4):
            hidden = hidden + own_ref[y, d].astype(F32)
        _, slope = gelu_parts(own_ref[d, 5])
        out_ref[d] = (hidden * slope).astype(BF)
        out_ref[4 + d] = own_ref[d, 4]


def part_kernel(pregrad_ref, own_ref, after_ref, far_ref, before_ref, out_ref, total, rows):
    total[...] = times_transposed(pregrad_ref[0], own_ref[...])
    total[...] += times_transposed(pregrad_ref[1], after_ref[...])
    total[...] += times_transposed(pregrad_ref[2], far_ref[...])
    total[...] += times_transposed(pregrad_ref[3], before_ref[...])
    for z in range(16):
        here = slice(12 * z, 12 * z + 12)
        rows[z, 0:12] = total[here, :512]
        rows[z, 12:24] = total[here, 512:]
        out_ref[z] = rows[z].astype(BF)


def times_tokens(a, b):
    return lax.dot_general(a, b, (((0,), (0,)), ((), ())), preferred_element_type=F32)


def weights_kernel(x_ref, own_ref, *refs):
    tokens, pregrad, (up_ref, down_ref) = refs[:4], (own_ref.at[0], *refs[4:7]), refs[7:]
    for d in range(4):
        up = times_tokens(tokens[d][1], pregrad[d][...])
        down = times_tokens(own_ref[4 + lax.rem(x_ref[0] + d, 4)], tokens[d][0])
        up_ref[...] = up if d == 0 else up_ref[...] + up
        down_ref[...] = down if d == 0 else down_ref[...] + down


def sum_kernel(part_ref, out_ref, rows):
    total = part_ref[0].astype(F32)
    for z in range(1, 16):
        total = total + part_ref[z].astype(F32)
    rows[...] = total
    out_ref[:, :512] = rows[0:12].astype(BF)
    out_ref[:, 512:] = rows[12:24].astype(BF)


def shift(k):
    return [(i, (i + k) % 4) for i in range(4)]


def near_x(block):
    return lax.ppermute(block, "x", shift(1)), lax.ppermute(block, "x", shift(-1))


def far_x(before, after):
    half = before.shape[0] // 2
    return lax.ppermute(before[:half], "x", shift(1)), lax.ppermute(after[half:], "x", shift(-1))


def local(inputs, out_grad, preact, up_weight, down_weight):
    core, at_x = lax.axis_index("c"), lax.axis_index("x")

    sixteen = jax.ShapeDtypeStruct((16, 48, 512), BF)
    (both,) = call(lay_out_kernel, [sixteen], [(48, 512)], 0, (out_grad, inputs))
    both = exchange(both, ("za", "zb"))
    swap = [(4 * a + b, 4 * ((b - a) % 4) + a) for a in range(4) for b in range(4)]
    turned = lax.ppermute(preact, ("y", "x"), swap)
    before, after = near_x(down_weight)
    far = far_x(before, after)
    up_before, up_after = near_x(up_weight)
    up_far = lax.ppermute(up_weight, "x", shift(2))
    both, before, after, far, up_before, up_after = lax.optimization_barrier(
        (both, before, after, far, up_before, up_after)
    )

    half = jax.ShapeDtypeStruct((4, 96, 256), F32)
    mine, theirs, tokens = call(
        hidden_kernel,
        [half, half, jax.ShapeDtypeStruct((2, 192, 1024), BF)],
        [(16, 48, 512), (192, 1024), (192, 1024)],
        2 * 192 * 1024 * 1024,
        (core[None], both, down_weight, after, *far, before),
        smem=1,
    )
    theirs, turned, up_far = lax.optimization_barrier((theirs, turned, up_far))
    theirs = lax.ppermute(theirs, "c", [(0, 1), (1, 0)])
    (own,) = call(payload_kernel, [jax.ShapeDtypeStruct((4, 6, 96, 256), BF)], [], 0, (mine, theirs, preact, turned))
    own = exchange(own, "y")
    (own,) = call(slope_kernel, [jax.ShapeDtypeStruct((8, 96, 256), BF)], [], 0, (own,))
    own = lax.all_gather(own, "c", axis=1, tiled=False).reshape(8, 192, 256)

    (part,) = call(
        part_kernel,
        [jax.ShapeDtypeStruct((16, 24, 512), BF)],
        [(192, 1024), (16, 24, 512)],
        2 * 192 * 1024 * 1024,
        (own, up_weight, up_after, up_far, up_before),
    )
    part = exchange(part, ("za", "zb"))

    all_tokens = [tokens] + [lax.ppermute(tokens, "x", shift(k)) for k in (3, 2, 1)]
    all_pregrad = [lax.ppermute(own[k], "x", shift(k)) for k in (3, 2, 1)]
    up_grad, down_grad = call(
        weights_kernel,
        [jax.ShapeDtypeStruct((1024, 256), F32), jax.ShapeDtypeStruct((256, 1024), F32)],
        [],
        16 * 4 * 768 * 1024 * 256,
        (at_x[None], own, *all_tokens, *all_pregrad),
        smem=1,
    )
    part, up_grad, down_grad = lax.optimization_barrier((part, up_grad, down_grad))
    (input_grad,) = call(sum_kernel, [jax.ShapeDtypeStruct((12, 1024), BF)], [(24, 512)], 0, (part,))
    return (input_grad, up_grad, down_grad)


def solution(mesh):
    fine = Mesh(mesh.devices.reshape(4, 2, 4, 4, 4), ("y", "c", "x", "za", "zb"))
    tokens, width = ("x", "za", "zb"), ("y", "c")
    return jax.shard_map(
        local,
        mesh=fine,
        in_specs=(
            P(tokens, width),
            P(tokens, width),
            P(width, tokens),
            P(width, tokens),
            P(tokens, width),
        ),
        out_specs=(P(tokens, width), P(width, tokens), P(tokens, width)),
        check_vma=False,
    )
```

```python
import math

import jax
import jax.numpy as jnp
from jax import lax
from jax.experimental import pallas as pl
from jax.experimental.pallas import tpu as pltpu
from jax.sharding import Mesh, PartitionSpec as P

BF = jnp.bfloat16
F32 = jnp.float32


def gelu_parts(preact):
    value = preact.astype(F32)
    normal_cdf = 0.5 * (1.0 + jax.scipy.special.erf(value / math.sqrt(2.0)))
    density = jnp.exp(-0.5 * value * value) / math.sqrt(2.0 * math.pi)
    return (value * normal_cdf, normal_cdf + value * density)


def exchange(blocks, axis):
    return lax.all_to_all(blocks, axis, split_axis=0, concat_axis=0, tiled=False)


def call(body, outs, scratch, flops, operands, smem=0):
    moved = sum(a.size * a.dtype.itemsize for a in (*operands, *outs))
    spaces = [pltpu.SMEM] * smem + [pltpu.VMEM] * (len(operands) - smem)
    return pl.pallas_call(
        body,
        out_shape=outs,
        in_specs=[pl.BlockSpec(memory_space=space) for space in spaces],
        out_specs=[pl.BlockSpec(memory_space=pltpu.VMEM)] * len(outs),
        scratch_shapes=[pltpu.VMEM(shape, F32) for shape in scratch],
        cost_estimate=pl.CostEstimate(flops=flops, bytes_accessed=moved, transcendentals=0),
        compiler_params=pltpu.CompilerParams(vmem_limit_bytes=16 * 2**20),
    )(*operands)


def times_transposed(a, b):
    return lax.dot_general(a, b, (((1,), (1,)), ((), ())), preferred_element_type=F32)


def lay_out_kernel(grad_ref, in_ref, out_ref, rows):
    for k, ref in enumerate((grad_ref, in_ref)):
        block = ref[...].astype(F32)
        rows[24 * k : 24 * k + 12] = block[:, :512]
        rows[24 * k + 12 : 24 * k + 24] = block[:, 512:]
    block = rows[...].astype(BF)
    for z in range(16):
        out_ref[z] = block


def put_back(both_ref, start, rows, tokens):
    for z in range(16):
        rows[z] = both_ref[z].astype(F32)
        here = slice(12 * z, 12 * z + 12)
        tokens[here, :512] = rows[z, start : start + 12]
        tokens[here, 512:] = rows[z, start + 12 : start + 24]


def tokens_kernel(both_ref, tokens_ref, rows, tokens):
    for k in range(2):
        put_back(both_ref, 24 * k, rows, tokens)
        tokens_ref[k] = tokens[...].astype(BF)


def hidden_kernel(core_ref, both_ref, own_ref, after_ref, far0_ref, far1_ref, before_ref, *refs):
    mine_ref, theirs_ref, rows, grads = refs
    put_back(both_ref, 0, rows, grads)
    first = pl.multiple_of(core_ref[0] * 96, 96)
    second = pl.multiple_of(96 - core_ref[0] * 96, 96)
    for start, out_ref in ((second, theirs_ref), (first, mine_ref)):
        half = grads[pl.ds(start, 96)].astype(BF)
        out_ref[0] = times_transposed(half, own_ref[...])
        out_ref[1] = times_transposed(half, after_ref[...])
        out_ref[2, :, :128] = times_transposed(half, far0_ref[...])
        out_ref[2, :, 128:] = times_transposed(half, far1_ref[...])
        out_ref[3] = times_transposed(half, before_ref[...])


def payload_kernel(mine_ref, theirs_ref, preact_ref, turned_ref, out_ref):
    for k in range(6):
        if k < 4:
            block = (mine_ref[k] + theirs_ref[k]).astype(BF)
        else:
            block = gelu_parts(preact_ref[...])[0].astype(BF) if k == 4 else turned_ref[...]
        for y in range(4):
            out_ref[y, k] = block


def slope_kernel(own_ref, out_ref):
    for d in range(4):
        hidden = own_ref[0, d].astype(F32)
        for y in range(1, 4):
            hidden = hidden + own_ref[y, d].astype(F32)
        _, slope = gelu_parts(own_ref[d, 5])
        out_ref[d] = (hidden * slope).astype(BF)
        out_ref[4 + d] = own_ref[d, 4]


def part_kernel(pregrad_ref, own_ref, after_ref, far0_ref, far1_ref, before_ref, out_ref, total, rows):
    total[...] = times_transposed(pregrad_ref[0], own_ref[...])
    total[...] += times_transposed(pregrad_ref[1], after_ref[...])
    total[:, :512] += times_transposed(pregrad_ref[2], far0_ref[...])
    total[:, 512:] += times_transposed(pregrad_ref[2], far1_ref[...])
    total[...] += times_transposed(pregrad_ref[3], before_ref[...])
    for z in range(16):
        here = slice(12 * z, 12 * z + 12)
        rows[z, 0:12] = total[here, :512]
        rows[z, 12:24] = total[here, 512:]
        out_ref[z] = rows[z].astype(BF)


def times_tokens(a, b):
    return lax.dot_general(a, b, (((0,), (0,)), ((), ())), preferred_element_type=F32)


def weights_kernel(x_ref, own_ref, *refs):
    tokens, pregrad, (up_ref, down_ref) = refs[:4], (own_ref.at[0], *refs[4:7]), refs[7:]
    for d in range(4):
        up = times_tokens(tokens[d][1], pregrad[d][...])
        down = times_tokens(own_ref[4 + lax.rem(x_ref[0] + d, 4)], tokens[d][0])
        up_ref[...] = up if d == 0 else up_ref[...] + up
        down_ref[...] = down if d == 0 else down_ref[...] + down


def sum_kernel(part_ref, out_ref, rows):
    total = part_ref[0].astype(F32)
    for z in range(1, 16):
        total = total + part_ref[z].astype(F32)
    rows[...] = total
    out_ref[:, :512] = rows[0:12].astype(BF)
    out_ref[:, 512:] = rows[12:24].astype(BF)


def shift(k):
    return [(i, (i + k) % 4) for i in range(4)]


def near_x(block):
    return lax.ppermute(block, "x", shift(1)), lax.ppermute(block, "x", shift(-1))


def far_x(before, after):
    half = before.shape[0] // 2
    return lax.ppermute(before[:half], "x", shift(1)), lax.ppermute(after[half:], "x", shift(-1))


def local(inputs, out_grad, preact, up_weight, down_weight):
    core, at_x = lax.axis_index("c"), lax.axis_index("x")

    sixteen = jax.ShapeDtypeStruct((16, 48, 512), BF)
    (both,) = call(lay_out_kernel, [sixteen], [(48, 512)], 0, (out_grad, inputs))
    both = exchange(both, ("za", "zb"))
    swap = [(4 * a + b, 4 * ((b - a) % 4) + a) for a in range(4) for b in range(4)]
    turned = lax.ppermute(preact, ("y", "x"), swap)
    before, after = near_x(down_weight)
    far = far_x(before, after)
    up_before, up_after = near_x(up_weight)
    up_far = far_x(up_before, up_after)
    both, before, after, far, up_before, up_after = lax.optimization_barrier(
        (both, before, after, far, up_before, up_after)
    )

    half = jax.ShapeDtypeStruct((4, 96, 256), F32)
    mine, theirs = call(
        hidden_kernel,
        [half, half],
        [(16, 48, 512), (192, 1024)],
        2 * 192 * 1024 * 1024,
        (core[None], both, down_weight, after, *far, before),
        smem=1,
    )
    theirs, turned, up_far = lax.optimization_barrier((theirs, turned, up_far))
    theirs = lax.ppermute(theirs, "c", [(0, 1), (1, 0)])
    (own,) = call(payload_kernel, [jax.ShapeDtypeStruct((4, 6, 96, 256), BF)], [], 0, (mine, theirs, preact, turned))
    own = exchange(own, "y")
    (own,) = call(slope_kernel, [jax.ShapeDtypeStruct((8, 96, 256), BF)], [], 0, (own,))
    own = lax.all_gather(own, "c", axis=1, tiled=False).reshape(8, 192, 256)

    (part,) = call(
        part_kernel,
        [jax.ShapeDtypeStruct((16, 24, 512), BF)],
        [(192, 1024), (16, 24, 512)],
        2 * 192 * 1024 * 1024,
        (own, up_weight, up_after, *up_far, up_before),
    )
    part = exchange(part, ("za", "zb"))

    tokens = jax.ShapeDtypeStruct((2, 192, 1024), BF)
    (tokens,) = call(tokens_kernel, [tokens], [(16, 48, 512), (192, 1024)], 0, (both,))
    all_tokens = [tokens] + [lax.ppermute(tokens, "x", shift(k)) for k in (3, 2, 1)]
    all_pregrad = [lax.ppermute(own[k], "x", shift(k)) for k in (3, 2, 1)]
    up_grad, down_grad = call(
        weights_kernel,
        [jax.ShapeDtypeStruct((1024, 256), F32), jax.ShapeDtypeStruct((256, 1024), F32)],
        [],
        16 * 4 * 768 * 1024 * 256,
        (at_x[None], own, *all_tokens, *all_pregrad),
        smem=1,
    )
    part, up_grad, down_grad = lax.optimization_barrier((part, up_grad, down_grad))
    (input_grad,) = call(sum_kernel, [jax.ShapeDtypeStruct((12, 1024), BF)], [(24, 512)], 0, (part,))
    return (input_grad, up_grad, down_grad)


def solution(mesh):
    fine = Mesh(mesh.devices.reshape(4, 2, 4, 4, 4), ("y", "c", "x", "za", "zb"))
    tokens, width = ("x", "za", "zb"), ("y", "c")
    return jax.shard_map(
        local,
        mesh=fine,
        in_specs=(
            P(tokens, width),
            P(tokens, width),
            P(width, tokens),
            P(width, tokens),
            P(tokens, width),
        ),
        out_specs=(P(tokens, width), P(width, tokens), P(tokens, width)),
        check_vma=False,
    )
```

```python
import math

import jax
import jax.numpy as jnp
from jax import lax
from jax.experimental import pallas as pl
from jax.experimental.pallas import tpu as pltpu
from jax.sharding import Mesh, PartitionSpec as P

BF = jnp.bfloat16
F32 = jnp.float32


def gelu_parts(preact):
    value = preact.astype(F32)
    normal_cdf = 0.5 * (1.0 + jax.scipy.special.erf(value / math.sqrt(2.0)))
    density = jnp.exp(-0.5 * value * value) / math.sqrt(2.0 * math.pi)
    return (value * normal_cdf, normal_cdf + value * density)


def exchange(blocks, axis):
    return lax.all_to_all(blocks, axis, split_axis=0, concat_axis=0, tiled=False)


def call(body, outs, scratch, flops, operands, smem=0):
    moved = sum(a.size * a.dtype.itemsize for a in (*operands, *outs))
    spaces = [pltpu.SMEM] * smem + [pltpu.VMEM] * (len(operands) - smem)
    return pl.pallas_call(
        body,
        out_shape=outs,
        in_specs=[pl.BlockSpec(memory_space=space) for space in spaces],
        out_specs=[pl.BlockSpec(memory_space=pltpu.VMEM)] * len(outs),
        scratch_shapes=[pltpu.VMEM(shape, F32) for shape in scratch],
        cost_estimate=pl.CostEstimate(flops=flops, bytes_accessed=moved, transcendentals=0),
        compiler_params=pltpu.CompilerParams(vmem_limit_bytes=16 * 2**20),
    )(*operands)


def times_transposed(a, b):
    return lax.dot_general(a, b, (((1,), (1,)), ((), ())), preferred_element_type=F32)


def lay_out_kernel(grad_ref, in_ref, out_ref, rows):
    for k, ref in enumerate((grad_ref, in_ref)):
        block = ref[...].astype(F32)
        rows[24 * k : 24 * k + 12] = block[:, :512]
        rows[24 * k + 12 : 24 * k + 24] = block[:, 512:]
    block = rows[...].astype(BF)
    for z in range(16):
        out_ref[z] = block


def put_back(both_ref, start, rows, tokens):
    for z in range(16):
        rows[z] = both_ref[z].astype(F32)
        here = slice(12 * z, 12 * z + 12)
        tokens[here, :512] = rows[z, start : start + 12]
        tokens[here, 512:] = rows[z, start + 12 : start + 24]


def tokens_kernel(both_ref, tokens_ref, rows, tokens):
    for k in range(2):
        put_back(both_ref, 24 * k, rows, tokens)
        tokens_ref[k] = tokens[...].astype(BF)


def hidden_kernel(core_ref, both_ref, own_ref, after_ref, far_ref, before_ref, *refs):
    mine_ref, theirs_ref, rows, grads = refs
    put_back(both_ref, 0, rows, grads)
    first = pl.multiple_of(core_ref[0] * 96, 96)
    second = pl.multiple_of(96 - core_ref[0] * 96, 96)
    for start, out_ref in ((second, theirs_ref), (first, mine_ref)):
        half = grads[pl.ds(start, 96)].astype(BF)
        out_ref[0] = times_transposed(half, own_ref[...])
        out_ref[1] = times_transposed(half, after_ref[...])
        out_ref[2] = times_transposed(half, far_ref[...])
        out_ref[3] = times_transposed(half, before_ref[...])


def payload_kernel(mine_ref, theirs_ref, turned_ref, out_ref):
    for k in range(5):
        block = (mine_ref[k] + theirs_ref[k]).astype(BF) if k < 4 else turned_ref[...]
        for y in range(4):
            out_ref[y, k] = block


def slope_kernel(own_ref, out_ref):
    for d in range(4):
        hidden = own_ref[0, d].astype(F32)
        for y in range(1, 4):
            hidden = hidden + own_ref[y, d].astype(F32)
        activ, slope = gelu_parts(own_ref[d, 4])
        out_ref[2 * d] = (hidden * slope).astype(BF)
        out_ref[2 * d + 1] = activ.astype(BF)


def part_kernel(pregrad_ref, own_ref, after_ref, far_ref, before_ref, out_ref, total, rows):
    total[...] = times_transposed(pregrad_ref[0, 0], own_ref[...])
    total[...] += times_transposed(pregrad_ref[1, 0], after_ref[...])
    total[...] += times_transposed(pregrad_ref[2, 0], far_ref[...])
    total[...] += times_transposed(pregrad_ref[3, 0], before_ref[...])
    for z in range(16):
        here = slice(12 * z, 12 * z + 12)
        rows[z, 0:12] = total[here, :512]
        rows[z, 12:24] = total[here, 512:]
        out_ref[z] = rows[z].astype(BF)


def times_tokens(a, b):
    return lax.dot_general(a, b, (((0,), (0,)), ((), ())), preferred_element_type=F32)


def weights_kernel(own_ref, *refs):
    tokens, units, (up_ref, down_ref) = refs[:4], (own_ref.at[0], *refs[4:7]), refs[7:]
    for d in range(4):
        up = times_tokens(tokens[d][1], units[d][0])
        down = times_tokens(units[d][1], tokens[d][0])
        up_ref[...] = up if d == 0 else up_ref[...] + up
        down_ref[...] = down if d == 0 else down_ref[...] + down


def sum_kernel(part_ref, out_ref, rows):
    total = part_ref[0].astype(F32)
    for z in range(1, 16):
        total = total + part_ref[z].astype(F32)
    rows[...] = total
    out_ref[:, :512] = rows[0:12].astype(BF)
    out_ref[:, 512:] = rows[12:24].astype(BF)


def shift(k):
    return [(i, (i + k) % 4) for i in range(4)]


def near_x(block):
    return lax.ppermute(block, "x", shift(1)), lax.ppermute(block, "x", shift(-1))


def local(inputs, out_grad, preact, up_weight, down_weight):
    core = lax.axis_index("c")

    sixteen = jax.ShapeDtypeStruct((16, 48, 512), BF)
    (both,) = call(lay_out_kernel, [sixteen], [(48, 512)], 0, (out_grad, inputs))
    both = exchange(both, ("za", "zb"))
    swap = [(4 * a + b, 4 * ((b - a) % 4) + a) for a in range(4) for b in range(4)]
    turned = lax.ppermute(preact, ("y", "x"), swap)
    before, after = near_x(down_weight)
    far = lax.ppermute(before, "x", shift(1))
    up_before, up_after = near_x(up_weight)
    up_far = lax.ppermute(up_after, "x", shift(-1))
    both, before, after, far, up_before, up_after = lax.optimization_barrier(
        (both, before, after, far, up_before, up_after)
    )

    half = jax.ShapeDtypeStruct((4, 96, 256), F32)
    mine, theirs = call(
        hidden_kernel,
        [half, half],
        [(16, 48, 512), (192, 1024)],
        2 * 192 * 1024 * 1024,
        (core[None], both, down_weight, after, far, before),
        smem=1,
    )
    theirs, turned, up_far = lax.optimization_barrier((theirs, turned, up_far))
    theirs = lax.ppermute(theirs, "c", [(0, 1), (1, 0)])
    (own,) = call(payload_kernel, [jax.ShapeDtypeStruct((4, 5, 96, 256), BF)], [], 0, (mine, theirs, turned))
    own = exchange(own, "y")
    (own,) = call(slope_kernel, [jax.ShapeDtypeStruct((8, 96, 256), BF)], [], 0, (own,))
    own = lax.all_gather(own, "c", axis=1, tiled=False).reshape(4, 2, 192, 256)

    (part,) = call(
        part_kernel,
        [jax.ShapeDtypeStruct((16, 24, 512), BF)],
        [(192, 1024), (16, 24, 512)],
        2 * 192 * 1024 * 1024,
        (own, up_weight, up_after, up_far, up_before),
    )
    part = exchange(part, ("za", "zb"))

    tokens = jax.ShapeDtypeStruct((2, 192, 1024), BF)
    (tokens,) = call(tokens_kernel, [tokens], [(16, 48, 512), (192, 1024)], 0, (both,))
    all_tokens = [tokens] + [lax.ppermute(tokens, "x", shift(k)) for k in (3, 2, 1)]
    all_units = [lax.ppermute(own[k], "x", shift(k)) for k in (3, 2, 1)]
    up_grad, down_grad = call(
        weights_kernel,
        [jax.ShapeDtypeStruct((1024, 256), F32), jax.ShapeDtypeStruct((256, 1024), F32)],
        [],
        16 * 4 * 768 * 1024 * 256,
        (own, *all_tokens, *all_units),
    )
    part, up_grad, down_grad = lax.optimization_barrier((part, up_grad, down_grad))
    (input_grad,) = call(sum_kernel, [jax.ShapeDtypeStruct((12, 1024), BF)], [(24, 512)], 0, (part,))
    return (input_grad, up_grad, down_grad)


def solution(mesh):
    fine = Mesh(mesh.devices.reshape(4, 2, 4, 4, 4), ("y", "c", "x", "za", "zb"))
    tokens, width = ("x", "za", "zb"), ("y", "c")
    return jax.shard_map(
        local,
        mesh=fine,
        in_specs=(
            P(tokens, width),
            P(tokens, width),
            P(width, tokens),
            P(width, tokens),
            P(tokens, width),
        ),
        out_specs=(P(tokens, width), P(width, tokens), P(tokens, width)),
        check_vma=False,
    )
```

```python
import math

import jax
import jax.numpy as jnp
from jax import lax
from jax.experimental import pallas as pl
from jax.experimental.pallas import tpu as pltpu
from jax.sharding import Mesh, PartitionSpec as P

BF = jnp.bfloat16
F32 = jnp.float32


def gelu_parts(preact):
    value = preact.astype(F32)
    normal_cdf = 0.5 * (1.0 + jax.scipy.special.erf(value / math.sqrt(2.0)))
    density = jnp.exp(-0.5 * value * value) / math.sqrt(2.0 * math.pi)
    return (value * normal_cdf, normal_cdf + value * density)


def exchange(blocks, axis):
    return lax.all_to_all(blocks, axis, split_axis=0, concat_axis=0, tiled=False)


def call(body, outs, scratch, flops, operands, smem=0):
    moved = sum(a.size * a.dtype.itemsize for a in (*operands, *outs))
    spaces = [pltpu.SMEM] * smem + [pltpu.VMEM] * (len(operands) - smem)
    return pl.pallas_call(
        body,
        out_shape=outs,
        in_specs=[pl.BlockSpec(memory_space=space) for space in spaces],
        out_specs=[pl.BlockSpec(memory_space=pltpu.VMEM)] * len(outs),
        scratch_shapes=[pltpu.VMEM(shape, F32) for shape in scratch],
        cost_estimate=pl.CostEstimate(flops=flops, bytes_accessed=moved, transcendentals=0),
        compiler_params=pltpu.CompilerParams(vmem_limit_bytes=16 * 2**20),
    )(*operands)


def times_transposed(a, b):
    return lax.dot_general(a, b, (((1,), (1,)), ((), ())), preferred_element_type=F32)


def lay_out_kernel(grad_ref, in_ref, out_ref, rows):
    for k, ref in enumerate((grad_ref, in_ref)):
        block = ref[...].astype(F32)
        rows[24 * k : 24 * k + 12] = block[:, :512]
        rows[24 * k + 12 : 24 * k + 24] = block[:, 512:]
    block = rows[...].astype(BF)
    for z in range(16):
        out_ref[z] = block


def put_back(both_ref, start, rows, tokens):
    for z in range(16):
        rows[z] = both_ref[z].astype(F32)
        here = slice(12 * z, 12 * z + 12)
        tokens[here, :512] = rows[z, start : start + 12]
        tokens[here, 512:] = rows[z, start + 12 : start + 24]


def tokens_kernel(both_ref, tokens_ref, rows, tokens):
    for k in range(2):
        put_back(both_ref, 24 * k, rows, tokens)
        tokens_ref[k] = tokens[...].astype(BF)


def hidden_kernel(core_ref, both_ref, own_ref, after_ref, far_ref, before_ref, *refs):
    mine_ref, theirs_ref, rows, grads = refs
    put_back(both_ref, 0, rows, grads)
    first = pl.multiple_of(core_ref[0] * 96, 96)
    second = pl.multiple_of(96 - core_ref[0] * 96, 96)
    for start, out_ref in ((second, theirs_ref), (first, mine_ref)):
        half = grads[pl.ds(start, 96)].astype(BF)
        out_ref[0] = times_transposed(half, own_ref[...])
        out_ref[1] = times_transposed(half, after_ref[...])
        out_ref[2] = times_transposed(half, far_ref[...])
        out_ref[3] = times_transposed(half, before_ref[...])


def payload_kernel(mine_ref, theirs_ref, turned_ref, out_ref):
    for k in range(5):
        block = (mine_ref[k] + theirs_ref[k]).astype(BF) if k < 4 else turned_ref[...]
        for y in range(4):
            out_ref[y, k] = block


def slope_kernel(own_ref, out_ref):
    for d in range(4):
        hidden = own_ref[0, d].astype(F32)
        for y in range(1, 4):
            hidden = hidden + own_ref[y, d].astype(F32)
        activ, slope = gelu_parts(own_ref[d, 4])
        out_ref[2 * d] = (hidden * slope).astype(BF)
        out_ref[2 * d + 1] = activ.astype(BF)


def part_kernel(pregrad_ref, own_ref, after_ref, far_ref, before_ref, out_ref, total, rows):
    total[...] = times_transposed(pregrad_ref[0, 0], own_ref[...])
    total[...] += times_transposed(pregrad_ref[1, 0], after_ref[...])
    total[...] += times_transposed(pregrad_ref[2, 0], far_ref[...])
    total[...] += times_transposed(pregrad_ref[3, 0], before_ref[...])
    for z in range(16):
        here = slice(12 * z, 12 * z + 12)
        rows[z, 0:12] = total[here, :512]
        rows[z, 12:24] = total[here, 512:]
        out_ref[z] = rows[z].astype(BF)


def times_tokens(a, b):
    return lax.dot_general(a, b, (((0,), (0,)), ((), ())), preferred_element_type=F32)


def weights_kernel(own_ref, *refs):
    tokens, units, (up_ref, down_ref) = refs[:4], (own_ref.at[0], *refs[4:7]), refs[7:]
    pregrad = jnp.concatenate([ref[0] for ref in units])
    activ = jnp.concatenate([ref[1] for ref in units])
    for part in range(4):
        here = slice(256 * part, 256 * part + 256)
        up_ref[here] = times_tokens(jnp.concatenate([ref[1, :, here] for ref in tokens]), pregrad)
        down_ref[:, here] = times_tokens(activ, jnp.concatenate([ref[0, :, here] for ref in tokens]))


def sum_kernel(part_ref, out_ref, rows):
    total = part_ref[0].astype(F32)
    for z in range(1, 16):
        total = total + part_ref[z].astype(F32)
    rows[...] = total
    out_ref[:, :512] = rows[0:12].astype(BF)
    out_ref[:, 512:] = rows[12:24].astype(BF)


def shift(k):
    return [(i, (i + k) % 4) for i in range(4)]


def near_x(block):
    return lax.ppermute(block, "x", shift(1)), lax.ppermute(block, "x", shift(-1))


def local(inputs, out_grad, preact, up_weight, down_weight):
    core = lax.axis_index("c")

    sixteen = jax.ShapeDtypeStruct((16, 48, 512), BF)
    (both,) = call(lay_out_kernel, [sixteen], [(48, 512)], 0, (out_grad, inputs))
    both = exchange(both, ("za", "zb"))
    swap = [(4 * a + b, 4 * ((b - a) % 4) + a) for a in range(4) for b in range(4)]
    turned = lax.ppermute(preact, ("y", "x"), swap)
    before, after = near_x(down_weight)
    far = lax.ppermute(before, "x", shift(1))
    up_before, up_after = near_x(up_weight)
    up_far = lax.ppermute(up_after, "x", shift(-1))
    both, before, after, far, up_after = lax.optimization_barrier((both, before, after, far, up_after))

    half = jax.ShapeDtypeStruct((4, 96, 256), F32)
    mine, theirs = call(
        hidden_kernel,
        [half, half],
        [(16, 48, 512), (192, 1024)],
        2 * 192 * 1024 * 1024,
        (core[None], both, down_weight, after, far, before),
        smem=1,
    )
    theirs, turned, up_before, up_far = lax.optimization_barrier((theirs, turned, up_before, up_far))
    theirs = lax.ppermute(theirs, "c", [(0, 1), (1, 0)])
    (own,) = call(payload_kernel, [jax.ShapeDtypeStruct((4, 5, 96, 256), BF)], [], 0, (mine, theirs, turned))
    own = exchange(own, "y")
    (own,) = call(slope_kernel, [jax.ShapeDtypeStruct((8, 96, 256), BF)], [], 0, (own,))
    own = lax.all_gather(own, "c", axis=1, tiled=False).reshape(4, 2, 192, 256)

    (part,) = call(
        part_kernel,
        [jax.ShapeDtypeStruct((16, 24, 512), BF)],
        [(192, 1024), (16, 24, 512)],
        2 * 192 * 1024 * 1024,
        (own, up_weight, up_after, up_far, up_before),
    )
    part = exchange(part, ("za", "zb"))

    tokens = jax.ShapeDtypeStruct((2, 192, 1024), BF)
    (tokens,) = call(tokens_kernel, [tokens], [(16, 48, 512), (192, 1024)], 0, (both,))
    all_tokens = [tokens] + [lax.ppermute(tokens, "x", shift(k)) for k in (3, 2, 1)]
    all_units = [lax.ppermute(own[k], "x", shift(k)) for k in (3, 2, 1)]
    up_grad, down_grad = call(
        weights_kernel,
        [jax.ShapeDtypeStruct((1024, 256), F32), jax.ShapeDtypeStruct((256, 1024), F32)],
        [],
        16 * 4 * 768 * 1024 * 256,
        (own, *all_tokens, *all_units),
    )
    part, up_grad, down_grad = lax.optimization_barrier((part, up_grad, down_grad))
    (input_grad,) = call(sum_kernel, [jax.ShapeDtypeStruct((12, 1024), BF)], [(24, 512)], 0, (part,))
    return (input_grad, up_grad, down_grad)


def solution(mesh):
    fine = Mesh(mesh.devices.reshape(4, 2, 4, 4, 4), ("y", "c", "x", "za", "zb"))
    tokens, width = ("x", "za", "zb"), ("y", "c")
    return jax.shard_map(
        local,
        mesh=fine,
        in_specs=(
            P(tokens, width),
            P(tokens, width),
            P(width, tokens),
            P(width, tokens),
            P(tokens, width),
        ),
        out_specs=(P(tokens, width), P(width, tokens), P(tokens, width)),
        check_vma=False,
    )
```

```python
import math

import jax
import jax.numpy as jnp
from jax import lax
from jax.experimental import pallas as pl
from jax.experimental.pallas import tpu as pltpu
from jax.sharding import Mesh, PartitionSpec as P

BF = jnp.bfloat16
F32 = jnp.float32


def gelu_parts(preact):
    value = preact.astype(F32)
    normal_cdf = 0.5 * (1.0 + jax.scipy.special.erf(value / math.sqrt(2.0)))
    density = jnp.exp(-0.5 * value * value) / math.sqrt(2.0 * math.pi)
    return (value * normal_cdf, normal_cdf + value * density)


def exchange(blocks, axis):
    return lax.all_to_all(blocks, axis, split_axis=0, concat_axis=0, tiled=False)


def call(body, outs, scratch, flops, operands, smem=0):
    moved = sum(a.size * a.dtype.itemsize for a in (*operands, *outs))
    spaces = [pltpu.SMEM] * smem + [pltpu.VMEM] * (len(operands) - smem)
    return pl.pallas_call(
        body,
        out_shape=outs,
        in_specs=[pl.BlockSpec(memory_space=space) for space in spaces],
        out_specs=[pl.BlockSpec(memory_space=pltpu.VMEM)] * len(outs),
        scratch_shapes=[pltpu.VMEM(shape, F32) for shape in scratch],
        cost_estimate=pl.CostEstimate(flops=flops, bytes_accessed=moved, transcendentals=0),
        compiler_params=pltpu.CompilerParams(vmem_limit_bytes=16 * 2**20),
    )(*operands)


def times_transposed(a, b):
    return lax.dot_general(a, b, (((1,), (1,)), ((), ())), preferred_element_type=F32)


def lay_out_kernel(grad_ref, in_ref, out_ref, rows):
    for k, ref in enumerate((grad_ref, in_ref)):
        block = ref[...].astype(F32)
        rows[24 * k : 24 * k + 12] = block[:, :512]
        rows[24 * k + 12 : 24 * k + 24] = block[:, 512:]
    block = rows[...].astype(BF)
    for z in range(16):
        out_ref[z] = block


def put_back(both_ref, start, rows, tokens):
    for z in range(16):
        rows[z] = both_ref[z].astype(F32)
        here = slice(12 * z, 12 * z + 12)
        tokens[here, :512] = rows[z, start : start + 12]
        tokens[here, 512:] = rows[z, start + 12 : start + 24]


def tokens_kernel(both_ref, tokens_ref, rows, tokens):
    for k in range(2):
        put_back(both_ref, 24 * k, rows, tokens)
        tokens_ref[k] = tokens[...].astype(BF)


def products(half, weights, out_ref):
    for d, ref in enumerate(weights):
        out_ref[d] = times_transposed(half, ref[...])


def theirs_kernel(core_ref, both_ref, own_ref, after_ref, far_ref, before_ref, *refs):
    theirs_ref, half_ref, rows, grads = refs
    put_back(both_ref, 0, rows, grads)
    half_ref[...] = grads[pl.ds(pl.multiple_of(core_ref[0] * 96, 96), 96)].astype(BF)
    theirs = grads[pl.ds(pl.multiple_of(96 - core_ref[0] * 96, 96), 96)].astype(BF)
    products(theirs, (own_ref, after_ref, far_ref, before_ref), theirs_ref)


def mine_kernel(half_ref, own_ref, after_ref, far_ref, before_ref, mine_ref):
    products(half_ref[...], (own_ref, after_ref, far_ref, before_ref), mine_ref)


def payload_kernel(mine_ref, theirs_ref, turned_ref, out_ref):
    for k in range(5):
        block = (mine_ref[k] + theirs_ref[k]).astype(BF) if k < 4 else turned_ref[...]
        for y in range(4):
            out_ref[y, k] = block


def slope_kernel(own_ref, out_ref):
    for d in range(4):
        hidden = own_ref[0, d].astype(F32)
        for y in range(1, 4):
            hidden = hidden + own_ref[y, d].astype(F32)
        activ, slope = gelu_parts(own_ref[d, 4])
        out_ref[2 * d] = (hidden * slope).astype(BF)
        out_ref[2 * d + 1] = activ.astype(BF)


def part_kernel(pregrad_ref, own_ref, after_ref, far_ref, before_ref, out_ref, total, rows):
    total[...] = times_transposed(pregrad_ref[0, 0], own_ref[...])
    total[...] += times_transposed(pregrad_ref[1, 0], after_ref[...])
    total[...] += times_transposed(pregrad_ref[2, 0], far_ref[...])
    total[...] += times_transposed(pregrad_ref[3, 0], before_ref[...])
    for z in range(16):
        here = slice(12 * z, 12 * z + 12)
        rows[z, 0:12] = total[here, :512]
        rows[z, 12:24] = total[here, 512:]
        out_ref[z] = rows[z].astype(BF)


def times_tokens(a, b):
    return lax.dot_general(a, b, (((0,), (0,)), ((), ())), preferred_element_type=F32)


def weights_kernel(own_ref, *refs):
    tokens, units, (up_ref, down_ref) = refs[:4], (own_ref.at[0], *refs[4:7]), refs[7:]
    pregrad = jnp.concatenate([ref[0] for ref in units])
    activ = jnp.concatenate([ref[1] for ref in units])
    for part in range(4):
        here = slice(256 * part, 256 * part + 256)
        up_ref[here] = times_tokens(jnp.concatenate([ref[1, :, here] for ref in tokens]), pregrad)
        down_ref[:, here] = times_tokens(activ, jnp.concatenate([ref[0, :, here] for ref in tokens]))


def sum_kernel(part_ref, out_ref, rows):
    total = part_ref[0].astype(F32)
    for z in range(1, 16):
        total = total + part_ref[z].astype(F32)
    rows[...] = total
    out_ref[:, :512] = rows[0:12].astype(BF)
    out_ref[:, 512:] = rows[12:24].astype(BF)


def shift(k):
    return [(i, (i + k) % 4) for i in range(4)]


def near_x(block):
    return lax.ppermute(block, "x", shift(1)), lax.ppermute(block, "x", shift(-1))


def local(inputs, out_grad, preact, up_weight, down_weight):
    core = lax.axis_index("c")

    sixteen = jax.ShapeDtypeStruct((16, 48, 512), BF)
    (both,) = call(lay_out_kernel, [sixteen], [(48, 512)], 0, (out_grad, inputs))
    both = exchange(both, ("za", "zb"))
    swap = [(4 * a + b, 4 * ((b - a) % 4) + a) for a in range(4) for b in range(4)]
    turned = lax.ppermute(preact, ("y", "x"), swap)
    before, after = near_x(down_weight)
    far = lax.ppermute(before, "x", shift(1))
    up_before, up_after = near_x(up_weight)
    up_far = lax.ppermute(up_after, "x", shift(-1))
    both, before, after, far, up_before, up_after = lax.optimization_barrier(
        (both, before, after, far, up_before, up_after)
    )

    half = jax.ShapeDtypeStruct((4, 96, 256), F32)
    weights = (down_weight, after, far, before)
    theirs, own_half = call(
        theirs_kernel,
        [half, jax.ShapeDtypeStruct((96, 1024), BF)],
        [(16, 48, 512), (192, 1024)],
        2 * 96 * 1024 * 1024,
        (core[None], both, *weights),
        smem=1,
    )
    (mine,) = call(mine_kernel, [half], [], 2 * 96 * 1024 * 1024, (own_half, *weights))
    theirs, turned, up_far = lax.optimization_barrier((theirs, turned, up_far))
    theirs = lax.ppermute(theirs, "c", [(0, 1), (1, 0)])
    (own,) = call(payload_kernel, [jax.ShapeDtypeStruct((4, 5, 96, 256), BF)], [], 0, (mine, theirs, turned))
    own = exchange(own, "y")
    (own,) = call(slope_kernel, [jax.ShapeDtypeStruct((8, 96, 256), BF)], [], 0, (own,))
    own = lax.all_gather(own, "c", axis=1, tiled=False).reshape(4, 2, 192, 256)

    (part,) = call(
        part_kernel,
        [jax.ShapeDtypeStruct((16, 24, 512), BF)],
        [(192, 1024), (16, 24, 512)],
        2 * 192 * 1024 * 1024,
        (own, up_weight, up_after, up_far, up_before),
    )
    part = exchange(part, ("za", "zb"))

    tokens = jax.ShapeDtypeStruct((2, 192, 1024), BF)
    (tokens,) = call(tokens_kernel, [tokens], [(16, 48, 512), (192, 1024)], 0, (both,))
    all_tokens = [tokens] + [lax.ppermute(tokens, "x", shift(k)) for k in (3, 2, 1)]
    all_units = [lax.ppermute(own[k], "x", shift(k)) for k in (3, 2, 1)]
    up_grad, down_grad = call(
        weights_kernel,
        [jax.ShapeDtypeStruct((1024, 256), F32), jax.ShapeDtypeStruct((256, 1024), F32)],
        [],
        16 * 4 * 768 * 1024 * 256,
        (own, *all_tokens, *all_units),
    )
    part, up_grad, down_grad = lax.optimization_barrier((part, up_grad, down_grad))
    (input_grad,) = call(sum_kernel, [jax.ShapeDtypeStruct((12, 1024), BF)], [(24, 512)], 0, (part,))
    return (input_grad, up_grad, down_grad)


def solution(mesh):
    fine = Mesh(mesh.devices.reshape(4, 2, 4, 4, 4), ("y", "c", "x", "za", "zb"))
    tokens, width = ("x", "za", "zb"), ("y", "c")
    return jax.shard_map(
        local,
        mesh=fine,
        in_specs=(
            P(tokens, width),
            P(tokens, width),
            P(width, tokens),
            P(width, tokens),
            P(tokens, width),
        ),
        out_specs=(P(tokens, width), P(width, tokens), P(tokens, width)),
        check_vma=False,
    )
```

```python
import math

import jax
import jax.numpy as jnp
from jax import lax
from jax.experimental import pallas as pl
from jax.experimental.pallas import tpu as pltpu
from jax.sharding import Mesh, PartitionSpec as P

BF = jnp.bfloat16
F32 = jnp.float32


def gelu_parts(preact):
    value = preact.astype(F32)
    normal_cdf = 0.5 * (1.0 + jax.scipy.special.erf(value / math.sqrt(2.0)))
    density = jnp.exp(-0.5 * value * value) / math.sqrt(2.0 * math.pi)
    return (value * normal_cdf, normal_cdf + value * density)


def exchange(blocks, axis):
    return lax.all_to_all(blocks, axis, split_axis=0, concat_axis=0, tiled=False)


def call(body, outs, scratch, flops, operands, smem=0, copied=0):
    moved = sum(a.size * a.dtype.itemsize for a in (*operands, *outs))
    spaces = [pltpu.SMEM] * smem + [pltpu.VMEM] * (len(operands) - smem - copied) + [pl.ANY] * copied
    return pl.pallas_call(
        body,
        out_shape=outs,
        in_specs=[pl.BlockSpec(memory_space=space) for space in spaces],
        out_specs=[pl.BlockSpec(memory_space=pltpu.VMEM)] * len(outs),
        scratch_shapes=[pltpu.VMEM(shape, F32) for shape in scratch]
        + [pltpu.VMEM(a.shape, a.dtype) for a in operands[len(operands) - copied :]]
        + [pltpu.SemaphoreType.DMA] * copied,
        cost_estimate=pl.CostEstimate(flops=flops, bytes_accessed=moved, transcendentals=0),
        compiler_params=pltpu.CompilerParams(vmem_limit_bytes=16 * 2**20),
    )(*operands)


def times_transposed(a, b):
    return lax.dot_general(a, b, (((1,), (1,)), ((), ())), preferred_element_type=F32)


def lay_out_kernel(grad_ref, in_ref, out_ref, rows):
    for k, ref in enumerate((grad_ref, in_ref)):
        block = ref[...].astype(F32)
        rows[24 * k : 24 * k + 12] = block[:, :512]
        rows[24 * k + 12 : 24 * k + 24] = block[:, 512:]
    block = rows[...].astype(BF)
    for z in range(16):
        out_ref[z] = block


def put_back(both_ref, start, rows, tokens):
    for z in range(16):
        rows[z] = both_ref[z].astype(F32)
        here = slice(12 * z, 12 * z + 12)
        tokens[here, :512] = rows[z, start : start + 12]
        tokens[here, 512:] = rows[z, start + 12 : start + 24]


def tokens_kernel(both_ref, tokens_ref, rows, tokens):
    for k in range(2):
        put_back(both_ref, 24 * k, rows, tokens)
        tokens_ref[k] = tokens[...].astype(BF)


def products(half, weights, out_ref):
    for d, ref in enumerate(weights):
        out_ref[d] = times_transposed(half, ref[...])


def theirs_kernel(core_ref, both_ref, own_ref, after_ref, far_ref, before_ref, *refs):
    theirs_ref, half_ref, rows, grads = refs
    put_back(both_ref, 0, rows, grads)
    half_ref[...] = grads[pl.ds(pl.multiple_of(core_ref[0] * 96, 96), 96)].astype(BF)
    theirs = grads[pl.ds(pl.multiple_of(96 - core_ref[0] * 96, 96), 96)].astype(BF)
    products(theirs, (own_ref, after_ref, far_ref, before_ref), theirs_ref)


def mine_kernel(half_ref, own_ref, after_ref, far_ref, before_ref, mine_ref):
    products(half_ref[...], (own_ref, after_ref, far_ref, before_ref), mine_ref)


def payload_kernel(mine_ref, theirs_ref, turned_ref, out_ref):
    for k in range(5):
        block = (mine_ref[k] + theirs_ref[k]).astype(BF) if k < 4 else turned_ref[...]
        for y in range(4):
            out_ref[y, k] = block


def slope_kernel(own_ref, out_ref):
    for d in range(4):
        hidden = own_ref[0, d].astype(F32)
        for y in range(1, 4):
            hidden = hidden + own_ref[y, d].astype(F32)
        activ, slope = gelu_parts(own_ref[d, 4])
        out_ref[2 * d] = (hidden * slope).astype(BF)
        out_ref[2 * d + 1] = activ.astype(BF)


def part_kernel(pregrad_ref, own_ref, after_ref, far_ref, before_ref, out_ref, total, rows, *copies):
    blocks = copies[:4]
    moves = [
        pltpu.make_async_copy(*move)
        for move in zip((own_ref, after_ref, far_ref, before_ref), blocks, copies[4:])
    ]
    for move in moves:
        move.start()
    for d in range(4):
        moves[d].wait()
        product = times_transposed(pregrad_ref[d, 0], blocks[d][...])
        total[...] = product if d == 0 else total[...] + product
    for z in range(16):
        here = slice(12 * z, 12 * z + 12)
        rows[z, 0:12] = total[here, :512]
        rows[z, 12:24] = total[here, 512:]
        out_ref[z] = rows[z].astype(BF)


def times_tokens(a, b):
    return lax.dot_general(a, b, (((0,), (0,)), ((), ())), preferred_element_type=F32)


def weights_kernel(own_ref, *refs):
    tokens, units, (up_ref, down_ref) = refs[:4], (own_ref.at[0], *refs[4:7]), refs[7:]
    pregrad = jnp.concatenate([ref[0] for ref in units])
    activ = jnp.concatenate([ref[1] for ref in units])
    for part in range(4):
        here = slice(256 * part, 256 * part + 256)
        up_ref[here] = times_tokens(jnp.concatenate([ref[1, :, here] for ref in tokens]), pregrad)
        down_ref[:, here] = times_tokens(activ, jnp.concatenate([ref[0, :, here] for ref in tokens]))


def sum_kernel(part_ref, out_ref, rows):
    total = part_ref[0].astype(F32)
    for z in range(1, 16):
        total = total + part_ref[z].astype(F32)
    rows[...] = total
    out_ref[:, :512] = rows[0:12].astype(BF)
    out_ref[:, 512:] = rows[12:24].astype(BF)


def shift(k):
    return [(i, (i + k) % 4) for i in range(4)]


def near_x(block):
    return lax.ppermute(block, "x", shift(1)), lax.ppermute(block, "x", shift(-1))


def local(inputs, out_grad, preact, up_weight, down_weight):
    core = lax.axis_index("c")

    sixteen = jax.ShapeDtypeStruct((16, 48, 512), BF)
    (both,) = call(lay_out_kernel, [sixteen], [(48, 512)], 0, (out_grad, inputs))
    both = exchange(both, ("za", "zb"))
    swap = [(4 * a + b, 4 * ((b - a) % 4) + a) for a in range(4) for b in range(4)]
    turned = lax.ppermute(preact, ("y", "x"), swap)
    before, after = near_x(down_weight)
    far = lax.ppermute(before, "x", shift(1))
    up_before, up_after = near_x(up_weight)
    up_far = lax.ppermute(up_after, "x", shift(-1))
    both, before, after, far, up_before, up_after = lax.optimization_barrier(
        (both, before, after, far, up_before, up_after)
    )

    half = jax.ShapeDtypeStruct((4, 96, 256), F32)
    weights = (down_weight, after, far, before)
    theirs, own_half = call(
        theirs_kernel,
        [half, jax.ShapeDtypeStruct((96, 1024), BF)],
        [(16, 48, 512), (192, 1024)],
        2 * 96 * 1024 * 1024,
        (core[None], both, *weights),
        smem=1,
    )
    (mine,) = call(mine_kernel, [half], [], 2 * 96 * 1024 * 1024, (own_half, *weights))
    theirs, turned, up_far = lax.optimization_barrier((theirs, turned, up_far))
    theirs = lax.ppermute(theirs, "c", [(0, 1), (1, 0)])
    (own,) = call(payload_kernel, [jax.ShapeDtypeStruct((4, 5, 96, 256), BF)], [], 0, (mine, theirs, turned))
    own = exchange(own, "y")
    (own,) = call(slope_kernel, [jax.ShapeDtypeStruct((8, 96, 256), BF)], [], 0, (own,))
    own = lax.all_gather(own, "c", axis=1, tiled=False).reshape(4, 2, 192, 256)

    (part,) = call(
        part_kernel,
        [jax.ShapeDtypeStruct((16, 24, 512), BF)],
        [(192, 1024), (16, 24, 512)],
        2 * 192 * 1024 * 1024,
        (own, up_weight, up_after, up_far, up_before),
        copied=4,
    )
    part = exchange(part, ("za", "zb"))

    tokens = jax.ShapeDtypeStruct((2, 192, 1024), BF)
    (tokens,) = call(tokens_kernel, [tokens], [(16, 48, 512), (192, 1024)], 0, (both,))
    all_tokens = [tokens] + [lax.ppermute(tokens, "x", shift(k)) for k in (3, 2, 1)]
    all_units = [lax.ppermute(own[k], "x", shift(k)) for k in (3, 2, 1)]
    up_grad, down_grad = call(
        weights_kernel,
        [jax.ShapeDtypeStruct((1024, 256), F32), jax.ShapeDtypeStruct((256, 1024), F32)],
        [],
        16 * 4 * 768 * 1024 * 256,
        (own, *all_tokens, *all_units),
    )
    part, up_grad, down_grad = lax.optimization_barrier((part, up_grad, down_grad))
    (input_grad,) = call(sum_kernel, [jax.ShapeDtypeStruct((12, 1024), BF)], [(24, 512)], 0, (part,))
    return (input_grad, up_grad, down_grad)


def solution(mesh):
    fine = Mesh(mesh.devices.reshape(4, 2, 4, 4, 4), ("y", "c", "x", "za", "zb"))
    tokens, width = ("x", "za", "zb"), ("y", "c")
    return jax.shard_map(
        local,
        mesh=fine,
        in_specs=(
            P(tokens, width),
            P(tokens, width),
            P(width, tokens),
            P(width, tokens),
            P(tokens, width),
        ),
        out_specs=(P(tokens, width), P(width, tokens), P(tokens, width)),
        check_vma=False,
    )
```
